512 devices in a mesh: row: 16 (over y_lo, x), col: 32 (over z, y_hi, core).
Axes of the slice: x: 4, y: 8 (y_hi: 2, y_lo: 4; y = y_hi * 4 + y_lo), z: 8, core: 2. Of those that a mesh axis runs over, the one named last changes fastest.
Arguments:
- features: bfloat16 [65536, 1024], P(('row', 'col')), may hold values from -24 to 24
- degree: int32 [65536], P(('row', 'col')), may hold values from 16 to 128
- blocks: bfloat16 [16, 32, 72, 128, 128], P('row', 'col'), may hold values from 0 to 1
- coords: int32 [16, 32, 72], P('row', 'col'), may hold values from 0 to 511, as said below
- counts: int32 [16, 32], P('row', 'col'), may hold values from 18 to 72, as said below
- w_self: bfloat16 [1024, 256], replicated, may hold values from -0.1875 to 0.1875
- w_neigh: bfloat16 [1024, 256], replicated, may hold values from -0.1875 to 0.1875
- offset: bfloat16 [256], replicated, may hold values from -3 to 3
- cotangent: bfloat16 [65536, 256], P(('row', 'col')), may hold values from -6 to 6
Outputs:
- node_out: bfloat16 [65536, 256], P(('row', 'col'))
- feat_grad: bfloat16 [65536, 1024], P(('row', 'col'))
- self_grad: bfloat16 [1024, 256], replicated
- neigh_grad: bfloat16 [1024, 256], replicated
- offset_grad: float32 [256], replicated
The draws below stay inside these ranges and needn't reach their ends.
Inputs may be any that keep to these rules, and one draw needn't show every extreme that they name: `coords`: within each entry (a, b) all 72 coordinates differ; each is i * 16 + j with i < 32 and j < 16. `counts`: some device uses all 72 slots in every draw.
All inputs are finite; a program needn't handle non-finite values.
Results may differ from the reference program's by a relative error of at most 0.022.
Values may be sent and summed in bfloat16 or wider, within the bound.
A program may use at most 64 MiB of HBM per device.

```python
import math
import jax
import jax.numpy as jnp
from jax import lax

IN_WIDTH = 1024
OUT_WIDTH = 256
NODES_DEV = 128
BLOCK = 128
GRID_ROWS = 16
GRID_COLS = 32
NODES = 65536
BAND_ROWS = 4096
PANEL_ROWS = 2048
DEST_BLOCKS = 32
SRC_BLOCKS = 16
SLOTS = 72


def draw_coords(key, part):
    key = jax.random.fold_in(key, 11)
    keys = jax.random.split(key, GRID_ROWS * GRID_COLS)

    def one_device(device_key):
        return jax.random.permutation(device_key, DEST_BLOCKS * SRC_BLOCKS)[:SLOTS]
    values = jax.vmap(one_device)(keys)
    return values.reshape(GRID_ROWS, GRID_COLS, SLOTS).astype(jnp.int32)


def draw_counts(key, part):
    key = jax.random.fold_in(key, 12)
    first_key, second_key = jax.random.split(key)
    drawn = jax.random.randint(first_key, (GRID_ROWS * GRID_COLS,), SLOTS // 4, SLOTS + 1)
    full_device = jax.random.randint(second_key, (), 0, GRID_ROWS * GRID_COLS)
    places = jnp.arange(GRID_ROWS * GRID_COLS, dtype=jnp.int32)
    drawn = jnp.where(places == full_device, SLOTS, drawn)
    return drawn.reshape(GRID_ROWS, GRID_COLS).astype(jnp.int32)


def plant(result, key, smallest, largest):
    dims = result.shape
    index_at = [jax.random.randint(jax.random.fold_in(key, axis), (), 0, dims[axis]) for axis in range(len(dims))]
    result = result.at[tuple(index_at)].set(smallest)
    longest = dims.index(max(dims))
    index_at[longest] = (index_at[longest] + 1) % dims[longest]
    return result.at[tuple(index_at)].set(largest)


def with_spikes(array, rng, source, target, shards_of, factor):
    owner, partner = [(jnp.arange(array.shape[dim]) // (array.shape[dim] // shards_of)).reshape([-1 if axis == dim else 1 for axis in range(array.ndim)]) for dim in (source, target)]
    chosen = jax.random.permutation(rng, shards_of)[partner]
    strong = (owner == chosen) | (owner == (partner + shards_of // 2) % shards_of)
    return jnp.where(strong, factor * array, array)


def shard_levels(own_key, dims, cuts, low, high):
    def one(dim, shards_of):
        draws = jax.random.uniform(jax.random.fold_in(jax.random.fold_in(own_key, 6), dim), (shards_of,), jnp.float32, low / len(cuts), high / len(cuts))
        return jnp.repeat(jnp.exp(draws), dims[dim] // shards_of).reshape((-1,) + (1,) * (len(dims) - dim - 1))

    level = one(*cuts[0])
    for cut in cuts[1:]:
        level = level * one(*cut)
    return level


def normal_values(stream_key, shape, spread, reach, pieces=(), kind=jnp.bfloat16):
    result = spread * jax.random.normal(stream_key, shape, jnp.float32)
    if pieces:
        result = result * shard_levels(stream_key, shape, pieces, -0.22, 0.18)
    return jnp.clip(result, -reach, reach).astype(kind)


def bell_draw_with(rng, extent, spread, bound, cuts, heavy, held_as=jnp.bfloat16):
    array = spread * jax.random.normal(rng, extent, jnp.float32)
    if cuts:
        array = array * shard_levels(rng, extent, cuts, -0.22, 0.18)
    return jnp.clip(with_spikes(array, jax.random.fold_in(rng, 3), *heavy), -bound, bound).astype(held_as)


def setup_inputs(seed: int = 0) -> dict:
    streams_of = jax.random.split(jax.random.key(seed), 10)
    return {
        "features": bell_draw_with(streams_of[0], (NODES, IN_WIDTH), 1.0, 24.0, ((0, 512),), (0, 1, 512, 6.0)),
        "degree": plant(jax.random.randint(streams_of[1], (NODES,), 16, 129), jax.random.fold_in(streams_of[1], 1), 16, 128).astype(jnp.int32),
        "blocks": jnp.clip(1.0 * jax.random.uniform(streams_of[2], (GRID_ROWS, GRID_COLS, SLOTS, BLOCK, BLOCK), jnp.float32) ** shard_levels(streams_of[2], (GRID_ROWS, GRID_COLS, SLOTS, BLOCK, BLOCK), ((0, 16), (1, 32)), -0.2, 0.2), 0.0, 1.0).astype(jnp.bfloat16),
        "coords": draw_coords(jax.random.fold_in(streams_of[9], 71), 0),
        "counts": draw_counts(jax.random.fold_in(streams_of[9], 71), 0),
        "w_self": normal_values(streams_of[5], (IN_WIDTH, OUT_WIDTH), IN_WIDTH ** -0.5, 0.1875),
        "w_neigh": normal_values(streams_of[6], (IN_WIDTH, OUT_WIDTH), IN_WIDTH ** -0.5, 0.1875),
        "offset": normal_values(streams_of[7], (OUT_WIDTH,), 0.5, 3.0),
        "cotangent": normal_values(streams_of[8], (NODES, OUT_WIDTH), 1.0, 6.0, ((0, 512),)),
    }


def round_trip(values):
    return lax.optimization_barrier(values.astype(jnp.bfloat16)).astype(jnp.float32)

def reference(features, degree, blocks, coords, counts, w_self, w_neigh, offset, cotangent):
    row_grid = GRID_ROWS
    col_grid = GRID_COLS
    projected = jnp.dot(features, w_neigh, preferred_element_type=jnp.float32).astype(jnp.bfloat16)
    panels = projected.reshape(row_grid, col_grid, NODES_DEV, OUT_WIDTH).transpose(1, 0, 2, 3)
    panels = panels.reshape(col_grid, SRC_BLOCKS, BLOCK, OUT_WIDTH)
    dest_range = jnp.arange(DEST_BLOCKS, dtype=jnp.int32)
    src_range = jnp.arange(SRC_BLOCKS, dtype=jnp.int32)
    slot_range = jnp.arange(SLOTS, dtype=jnp.int32)

    def device_meta(row_idx, col_idx):
        codes = coords[row_idx, col_idx]
        filled = slot_range < counts[row_idx, col_idx]
        dest_idx = codes // SRC_BLOCKS
        src_idx = codes % SRC_BLOCKS
        dest_hot = ((dest_idx[None, :] == dest_range[:, None]) & filled[None, :]).astype(jnp.float32)
        src_hot = ((src_idx[None, :] == src_range[:, None]) & filled[None, :]).astype(jnp.float32)
        return (blocks[row_idx, col_idx].astype(jnp.float32), dest_idx, src_idx, dest_hot, src_hot)

    def forward_part(row_idx, col_idx):
        tiles, dest_idx, src_idx, dest_hot, src_hot = device_meta(row_idx, col_idx)
        picked = panels[col_idx][src_idx].astype(jnp.float32)
        products = jnp.einsum('kij,kjh->kih', tiles, picked)
        partial_value = jnp.einsum('dk,kih->dih', dest_hot, products, precision=lax.Precision.HIGHEST)
        return round_trip(partial_value.reshape(BAND_ROWS, OUT_WIDTH))

    def band_sum(row_idx):

        def step(total, col_idx):
            return (total + forward_part(row_idx, col_idx), None)
        start = jnp.zeros((BAND_ROWS, OUT_WIDTH), jnp.float32)
        return lax.scan(step, start, jnp.arange(col_grid, dtype=jnp.int32))[0]
    aggregate = lax.map(band_sum, jnp.arange(row_grid, dtype=jnp.int32)).reshape(NODES, OUT_WIDTH)
    degree_f = degree.astype(jnp.float32)[:, None]
    preact = jnp.dot(features, w_self, preferred_element_type=jnp.float32) + aggregate / degree_f + offset.astype(jnp.float32)[None, :]
    sigmoid_pre = jax.nn.sigmoid(preact)
    node_out = (preact * sigmoid_pre).astype(jnp.bfloat16)
    dpre = cotangent.astype(jnp.float32) * sigmoid_pre * (1.0 + preact * (1.0 - sigmoid_pre))
    dpre_b = dpre.astype(jnp.bfloat16)
    dscaled = (dpre / degree_f).astype(jnp.bfloat16)
    bands = dscaled.reshape(row_grid, DEST_BLOCKS, BLOCK, OUT_WIDTH)

    def backward_part(row_idx, col_idx):
        tiles, dest_idx, src_idx, dest_hot, src_hot = device_meta(row_idx, col_idx)
        chosen = bands[row_idx][dest_idx].astype(jnp.float32)
        products = jnp.einsum('kij,kih->kjh', tiles, chosen)
        returned = jnp.einsum('sk,kjh->sjh', src_hot, products, precision=lax.Precision.HIGHEST)
        return round_trip(returned.reshape(PANEL_ROWS, OUT_WIDTH))

    def panel_sum(col_idx):

        def step(total, row_idx):
            return (total + backward_part(row_idx, col_idx), None)
        start = jnp.zeros((PANEL_ROWS, OUT_WIDTH), jnp.float32)
        return lax.scan(step, start, jnp.arange(row_grid, dtype=jnp.int32))[0]
    dprop = lax.map(panel_sum, jnp.arange(col_grid, dtype=jnp.int32))
    dprop = dprop.reshape(col_grid, row_grid, NODES_DEV, OUT_WIDTH).transpose(1, 0, 2, 3).reshape(NODES, OUT_WIDTH)
    dprop_b = dprop.astype(jnp.bfloat16)
    feat_grad = (jnp.dot(dpre_b, w_self.T, preferred_element_type=jnp.float32) + jnp.dot(dprop_b, w_neigh.T, preferred_element_type=jnp.float32)).astype(jnp.bfloat16)
    grad_scale = 1.0 / math.sqrt(NODES)
    self_grad = (jnp.dot(features.T, dpre_b, preferred_element_type=jnp.float32) * grad_scale).astype(jnp.bfloat16)
    neigh_grad = (jnp.dot(features.T, dprop_b, preferred_element_type=jnp.float32) * grad_scale).astype(jnp.bfloat16)
    offset_grad = lax.optimization_barrier(jnp.sum(dpre, axis=0)) * grad_scale
    return (node_out, feat_grad, self_grad, neigh_grad, offset_grad)
```

```python
import functools
import math

import jax
import jax.numpy as jnp
from jax import lax
from jax.experimental import pallas as pl
from jax.experimental.pallas import tpu as pltpu
from jax.sharding import PartitionSpec as P

MESH = pl.DeviceIdType.MESH
BF16 = jnp.bfloat16
F32 = jnp.float32
X = 4
LANES = 128
BIG = 1 << 20


def spread_t(row):
    return jnp.broadcast_to(row, (LANES, LANES)).T


def slot_tables(group, other, used, slots):
    lane = lax.broadcasted_iota(jnp.int32, (LANES, LANES), 1)
    sub = lax.broadcasted_iota(jnp.int32, (LANES, LANES), 0)
    key = jnp.where(used > 0, group * LANES + lane[:1], BIG + lane[:1])
    key_r = jnp.broadcast_to(key, (LANES, LANES))
    key_c = spread_t(key)
    grp_r = jnp.broadcast_to(group, (LANES, LANES))
    grp_c = spread_t(group)
    used_c = spread_t(used)
    other_c = spread_t(other)
    less = jnp.where(key_r < key_c, 1, 0)
    rank = jnp.sum(less, axis=1, keepdims=True)
    same = jnp.where(grp_r == grp_c, less, 0)
    keep = jnp.minimum(jnp.sum(same, axis=1, keepdims=True), 1)
    hot = rank == lane
    order = jnp.sum(jnp.where(hot, sub, 0), axis=0, keepdims=True)
    there = jnp.sum(jnp.where(hot, other_c, 0), axis=0, keepdims=True)
    keeps = jnp.sum(jnp.where(hot, keep, 0), axis=0, keepdims=True)
    upto = jnp.sum(jnp.where(grp_c <= lane, used_c, 0), axis=0, keepdims=True)
    here = jnp.sum(jnp.where(grp_c == lane, used_c, 0), axis=0, keepdims=True)
    last = jnp.where(here > 0, upto - 1, slots)
    return [order, there, keeps, last]


def kernel(
    rows, cols, slots, scale,
    feat_ref, deg_ref, blocks_ref, coords_ref, counts_ref, ws_ref, wn_ref, off_ref, cot_ref,
    node_ref, fgrad_ref, sgrad_ref, ngrad_ref, ograd_ref,
    tiles, panel, sums, part, core_in, flow_out, flow_in, yh_out, yh_in, bands, back,
    ring_out, ring_in, line_out, line_in, own_pre, fsum,
    e1_out, e1_in, e2_out, e2_in, e3_out, e3_in, e4, egather, o1, o2, o3, o4,
    table_v, table_s, copy_sem, send_sem, recv_sem,
):
    yl_n = rows // X
    z_n = cols // 4
    half = z_n // 2
    row = lax.axis_index("row")
    col = lax.axis_index("col")
    x = lax.rem(row, X)
    yl = row // X
    z = col // 4
    yh = lax.rem(col // 2, 2)
    c = lax.rem(col, 2)
    src_n = rows
    dest_n = cols

    def at(yl_=None, x_=None, z_=None, yh_=None, c_=None):
        yl_ = yl if yl_ is None else yl_
        x_ = x if x_ is None else x_
        z_ = z if z_ is None else z_
        yh_ = yh if yh_ is None else yh_
        c_ = c if c_ is None else c_
        return (yl_ * X + x_, z_ * 4 + yh_ * 2 + c_)

    def turn(i, d, n):
        return lax.rem(i + (d % n), n)

    y_n = 2 * yl_n
    y = yh * yl_n + yl

    def at_y(y_):
        return at(yl_=lax.rem(y_, yl_n), yh_=y_ // yl_n)

    x_peers = [at(x_=turn(x, d, X)) for d in range(1, X)]
    z_peers = [at(z_=turn(z, d, z_n)) for d in range(1, z_n)]
    y_peers = [at_y(turn(y, d, y_n)) for d in range(1, y_n)]
    core_peer = at(c_=1 - c)
    peers = x_peers + z_peers + y_peers + [core_peer]

    issued = []

    def put(src, dst, device):
        i = len(issued)
        copy = pltpu.make_async_remote_copy(
            src_ref=src, dst_ref=dst, send_sem=send_sem.at[i], recv_sem=recv_sem.at[i],
            device_id=device, device_id_type=MESH,
        )
        copy.start()
        issued.append(copy)
        return copy

    def dot(a, b):
        return jnp.dot(a, b, preferred_element_type=F32)

    def dot_t(a, b):
        return lax.dot_general(a, b, (((0,), (0,)), ((), ())), preferred_element_type=F32)

    def dot_nt(a, b):
        return lax.dot_general(a, b, (((1,), (1,)), ((), ())), preferred_element_type=F32)

    load = pltpu.make_async_copy(blocks_ref, tiles, copy_sem.at[0])
    load.start()
    barrier = pltpu.get_barrier_semaphore()
    for peer in peers:
        pl.semaphore_signal(barrier, inc=1, device_id=peer, device_id_type=MESH)
    panel[x * yl_n + yl] = dot(feat_ref[...], wn_ref[...]).astype(BF16)
    pl.semaphore_wait(barrier, len(peers))

    mine = panel.at[x * yl_n + yl]
    a_line = {d: put(mine, mine, at(yl_=turn(yl, d, yl_n))) for d in range(1, yl_n)}
    right, left = at(x_=turn(x, 1, X)), at(x_=turn(x, -1, X))
    a_right, a_left = {}, {}
    for d in range(yl_n):
        if d > 0:
            a_line[d].wait_recv()
        ref = panel.at[x * yl_n + turn(yl, -d, yl_n)]
        a_right[d] = put(ref, ref, right)
        a_left[d] = put(ref, ref, left)
        if d == 0:
            table_v[...] = jnp.zeros_like(table_v)
            table_v[0:1, 0:slots] = coords_ref[...]
            code = table_v[0:1, :]
            lane = lax.broadcasted_iota(jnp.int32, (1, LANES), 1)
            used = jnp.where(lane < counts_ref[0, 0], 1, 0)
            src_bits = (src_n - 1).bit_length()
            dest = lax.shift_right_logical(code, src_bits)
            src = lax.bitwise_and(code, src_n - 1)
            dest_q = lax.bitwise_and(dest, 1) * (dest_n // 2) + lax.shift_right_logical(dest, 1)
            src_q = lax.bitwise_and(src, X - 1) * yl_n + lax.shift_right_logical(src, 2)
            lines = slot_tables(dest_q, src_q, used, slots)
            lines += slot_tables(src_q, dest_q, used, slots)
            for i, line in enumerate(lines):
                table_v[i:i + 1, :] = line
            table_copy = pltpu.make_async_copy(table_v, table_s, copy_sem.at[1])
            table_copy.start()
            own_pre[...] = dot(feat_ref[...], ws_ref[...]) + off_ref[...].astype(F32)
            sums[slots] = jnp.zeros_like(sums[slots])
    fwd = []
    for d in range(yl_n):
        a_right[d].wait_recv()
        if d % 2 == 0:
            ref = panel.at[turn(x, -1, X) * yl_n + turn(yl, -d, yl_n)]
            fwd.append(put(ref, ref, right))
        a_left[d].wait_recv()
        if d % 2 == 1:
            ref = panel.at[turn(x, 1, X) * yl_n + turn(yl, -d, yl_n)]
            fwd.append(put(ref, ref, left))
    table_copy.wait()
    load.wait()
    for copy in fwd:
        copy.wait_recv()

    def products(line, matrix, operand):
        def step(k, total):
            tile = tiles[table_s[line, k]]
            rows_in = operand[table_s[line + 1, k]]
            total = total * table_s[line + 2, k].astype(F32) + matrix(tile, rows_in)
            sums[k] = total.astype(BF16)
            return total
        lax.fori_loop(0, slots, step, jnp.zeros(sums.shape[1:], F32), unroll=4)

    products(0, dot, panel)

    reach = []
    for d in range(half, 0, -1):
        reach += [d, z_n - d] if z_n - d != d else [d]
    reach += [0]
    core_copy = {}
    for d in reach:
        zz = turn(z, d, z_n)
        for h in range(2):
            q = (1 - c) * (dest_n // 2) + zz * 2 + h
            part[q] = sums[table_s[3, q]]
        ref = part.at[pl.ds((1 - c) * (dest_n // 2) + zz * 2, 2)]
        core_copy[d] = put(ref, core_in.at[pl.ds(zz * 2, 2)], core_peer)
    def take(q, _):
        part[c * (dest_n // 2) + q] = sums[table_s[3, c * (dest_n // 2) + q]]
        return 0
    lax.fori_loop(0, dest_n // 2, take, 0)

    def own2(d, r):
        q = turn(z, d, z_n) * 2 + (yh if r == 0 else 1 - yh)
        return part[c * (dest_n // 2) + q].astype(F32) + core_in[q].astype(F32)

    z_right, z_left = at(z_=turn(z, 1, z_n)), at(z_=turn(z, -1, z_n))
    flows = [(1, 0, half), (-1, 1, half), (1, 1, half - 1), (-1, 0, half - 1)]
    flow_last = {}
    ready = set()
    slot = 0
    for step in range(half):
        for way, r, top in flows:
            d = top - step
            if d < 1:
                continue
            if (way * d) % z_n not in ready:
                core_copy[(way * d) % z_n].wait_recv()
                ready.add((way * d) % z_n)
            value = own2(way * d, r)
            if step > 0:
                copy, at_slot = flow_last[(way, r)]
                copy.wait_recv()
                value = value + flow_in[at_slot].astype(F32)
            flow_out[slot] = value.astype(BF16)
            copy = put(flow_out.at[slot], flow_in.at[slot], z_right if way == 1 else z_left)
            flow_last[(way, r)] = (copy, slot)
            slot += 1
    core_copy[0].wait_recv()

    def arrived(r):
        value = own2(0, r)
        for way in (1, -1):
            if (way, r) in flow_last:
                copy, at_slot = flow_last[(way, r)]
                copy.wait_recv()
                value = value + flow_in[at_slot].astype(F32)
        return value

    yh_out[...] = arrived(1).astype(BF16)
    yh_copy = put(yh_out, yh_in, at(yh_=1 - yh))
    mine_sum = arrived(0)
    yh_copy.wait_recv()
    aggregate = mine_sum + yh_in[...].astype(F32)

    deg = jnp.broadcast_to(deg_ref[...].astype(F32), (LANES, LANES)).T
    deg = jnp.concatenate([deg] * (aggregate.shape[1] // LANES), axis=1)
    preact = own_pre[...] + aggregate / deg
    sig = jax.nn.sigmoid(preact)
    dpre = cot_ref[...].astype(F32) * sig * (1.0 + preact * (1.0 - sig))
    dpre_b = dpre.astype(BF16)
    own_band = c * (dest_n // 2) + z * 2 + yh
    bands[own_band] = (dpre / deg).astype(BF16)

    def band(d, r):
        return bands.at[c * (dest_n // 2) + turn(z, d, z_n) * 2 + (yh if r == 0 else 1 - yh)]

    def pass_on(ref, way):
        return put(ref, ref, z_right if way == 1 else z_left)

    to_core = []
    c_yh = put(band(0, 0), band(0, 0), at(yh_=1 - yh))
    hops = {}
    for way in (1, -1):
        hops[(way, 0)] = pass_on(band(0, 0), way) if (way == 1 or half > 1) else None
    to_core.append(put(band(0, 0), band(0, 0), core_peer))
    node_ref[...] = (preact * sig).astype(BF16)

    piece = feat_ref.shape[1] // (2 * X * z_n)
    f_half = feat_ref.shape[1] // 2
    f_x = f_half // X

    def all_reduce(i, value, side):
        fsum[i] = value
        e1_out[i] = fsum[i, pl.ds((1 - c) * f_half, f_half)].astype(BF16)
        copy = put(e1_out.at[i], e1_in.at[i], core_peer)
        if side is not None:
            o1[c] = side
            o_copies = [put(o1.at[c], o1.at[c], core_peer)]
        yield
        copy.wait_recv()
        fsum[i, 0:f_half] = fsum[i, pl.ds(c * f_half, f_half)] + e1_in[i].astype(F32)
        e2_out[i] = fsum[i, 0:f_half].astype(BF16)
        copies = []
        for d in range(1, X):
            there = turn(x, d, X)
            copies.append(put(e2_out.at[i, pl.ds(there * f_x, f_x)], e2_in.at[i, d], at(x_=there)))
        if side is not None:
            for o_copy in o_copies:
                o_copy.wait_recv()
            o2[x] = jnp.sum(o1[...], axis=0)
            o_copies = [put(o2.at[x], o2.at[x], peer) for peer in x_peers]
        yield
        total = fsum[i, pl.ds(x * f_x, f_x)]
        for d in range(1, X):
            copies[d - 1].wait_recv()
            total = total + e2_in[i, d].astype(F32)
        fsum[i, 0:f_x] = total
        e3_out[i] = total.astype(BF16)
        copies = []
        for d in range(1, z_n):
            there = turn(z, d, z_n)
            copies.append(put(e3_out.at[i, pl.ds(there * piece, piece)], e3_in.at[i, d], at(z_=there)))
        if side is not None:
            for o_copy in o_copies:
                o_copy.wait_recv()
            o3[z] = jnp.sum(o2[...], axis=0)
            o_copies = [put(o3.at[z], o3.at[z], peer) for peer in z_peers]
        yield
        total = fsum[i, pl.ds(z * piece, piece)]
        for d in range(1, z_n):
            copies[d - 1].wait_recv()
            total = total + e3_in[i, d].astype(F32)
        e4[i, y] = total.astype(BF16)
        copies = [put(e4.at[i, y], e4.at[i, y], peer) for peer in y_peers]
        if side is not None:
            for o_copy in o_copies:
                o_copy.wait_recv()
            o4[y] = jnp.sum(o3[...], axis=0)
            o_copies = [put(o4.at[y], o4.at[y], peer) for peer in y_peers]
        yield
        for copy in copies:
            copy.wait_recv()
        total = e4[i, 0].astype(F32)
        for there in range(1, y_n):
            total = total + e4[i, there].astype(F32)
        start = c * f_half + x * f_x + z * piece
        egather[i, pl.ds(start, piece)] = (total * scale).astype(BF16)
        ref = egather.at[i, pl.ds(start, piece)]
        copies = [put(ref, ref, peer) for peer in z_peers]
        if side is not None:
            for o_copy in o_copies:
                o_copy.wait_recv()
            ograd_ref[...] = (jnp.sum(o4[...], axis=0) * scale)[0:1]
        yield
        for copy in copies:
            copy.wait_recv()
        ref = egather.at[i, pl.ds(c * f_half + x * f_x, f_x)]
        copies = [put(ref, ref, peer) for peer in x_peers]
        yield
        for copy in copies:
            copy.wait_recv()
        ref = egather.at[i, pl.ds(c * f_half, f_half)]
        copy = put(ref, ref, core_peer)
        yield
        copy.wait_recv()
        out = sgrad_ref if i == 0 else ngrad_ref
        out[...] = egather[i]

    side = jnp.broadcast_to(jnp.sum(dpre, axis=0, keepdims=True), o1.shape[1:])
    self_steps = all_reduce(0, dot_t(feat_ref[...], dpre_b), side)
    next(self_steps)

    c_yh.wait_recv()
    for way in (1, -1):
        hops[(way, 1)] = pass_on(band(0, 1), way) if (way == -1 or half > 1) else None
    to_core.append(put(band(0, 1), band(0, 1), core_peer))
    for dist in range(1, half + 1):
        for way, r in ((1, 0), (-1, 0), (1, 1), (-1, 1)):
            if hops.get((way, r)) is None:
                continue
            hops[(way, r)].wait_recv()
            ref = band(-way * dist, r)
            top = half if (way, r) in ((1, 0), (-1, 1)) else half - 1
            hops[(way, r)] = pass_on(ref, way) if dist < top else None
            to_core.append(put(ref, ref, core_peer))
        if dist == half // 2:
            next(self_steps)
    own_pre[...] = dpre
    for copy in to_core:
        copy.wait_recv()
    next(self_steps)

    products(4, dot_t, bands)

    def take_back(q, _):
        back[q] = sums[table_s[7, q]]
        return 0
    lax.fori_loop(0, src_n, take_back, 0)

    def back_at(dx, d):
        return turn(x, dx, X) * yl_n + turn(yl, d, yl_n)

    order = list(range(1, yl_n)) + [0]
    far = {}
    for d in order:
        way = 1 if d % 2 == 0 else -1
        far[d] = put(back.at[back_at(2, d)], ring_in.at[0, d], right if way == 1 else left)
    near = {}
    for d in order:
        for way in (1, -1):
            if (d % 2 == 0) != (way == 1):
                near[(way, d)] = put(
                    back.at[back_at(way, d)], ring_in.at[1 if way == 1 else 2, d], right if way == 1 else left
                )
    for d in order:
        way = 1 if d % 2 == 0 else -1
        far[d].wait_recv()
        ring_out[d] = (back[back_at(way, d)].astype(F32) + ring_in[0, d].astype(F32)).astype(BF16)
        near[(way, d)] = put(ring_out.at[d], ring_in.at[1 if way == 1 else 2, d], right if way == 1 else left)
    next(self_steps)
    y_copy = {}
    for d in order:
        near[(1, d)].wait_recv()
        near[(-1, d)].wait_recv()
        value = back[back_at(0, d)].astype(F32) + ring_in[1, d].astype(F32) + ring_in[2, d].astype(F32)
        if d > 0:
            line_out[d] = value.astype(BF16)
            y_copy[d] = put(line_out.at[d], line_in.at[d], at(yl_=turn(yl, d, yl_n)))
        else:
            dprop = value
    next(self_steps)
    for d in range(1, yl_n):
        y_copy[d].wait_recv()
        dprop = dprop + line_in[d].astype(F32)
    dprop_b = dprop.astype(BF16)

    neigh_steps = all_reduce(1, dot_t(feat_ref[...], dprop_b), None)
    next(neigh_steps)
    next(self_steps)
    fgrad_ref[...] = (
        dot_nt(own_pre[...].astype(BF16), ws_ref[...]) + dot_nt(dprop_b, wn_ref[...])
    ).astype(BF16)
    for step in neigh_steps:
        next(self_steps, None)
    for step in self_steps:
        pass
    for copy in issued:
        copy.wait_send()


def run(rows, cols, features, degree, blocks, coords, counts, w_self, w_neigh, offset, cotangent):
    nodes_dev, hidden = cotangent.shape
    width = features.shape[1]
    slots, side = blocks.shape[2], blocks.shape[3]
    z_n, yl_n = cols // 4, rows // X
    y_n = 2 * yl_n
    f_half = width // 2
    f_x = f_half // X
    piece = f_x // z_n
    scale = 1.0 / math.sqrt(nodes_dev * rows * cols)
    vmem = pl.BlockSpec(memory_space=pltpu.VMEM)
    block = (side, hidden)
    copies = 400
    scratch = [
        pltpu.VMEM((slots, side, side), BF16),
        pltpu.VMEM((rows,) + block, BF16),
        pltpu.VMEM((slots + 1,) + block, BF16),
        pltpu.VMEM((cols,) + block, BF16),
        pltpu.VMEM((cols // 2,) + block, BF16),
        pltpu.VMEM((2 * z_n,) + block, BF16),
        pltpu.VMEM((2 * z_n,) + block, BF16),
        pltpu.VMEM(block, BF16),
        pltpu.VMEM(block, BF16),
        pltpu.VMEM((cols,) + block, BF16),
        pltpu.VMEM((rows,) + block, BF16),
        pltpu.VMEM((yl_n,) + block, BF16),
        pltpu.VMEM((3, yl_n) + block, BF16),
        pltpu.VMEM((yl_n,) + block, BF16),
        pltpu.VMEM((yl_n,) + block, BF16),
        pltpu.VMEM((nodes_dev, hidden), F32),
        pltpu.VMEM((2, width, hidden), F32),
        pltpu.VMEM((2, f_half, hidden), BF16),
        pltpu.VMEM((2, f_half, hidden), BF16),
        pltpu.VMEM((2, f_half, hidden), BF16),
        pltpu.VMEM((2, X, f_x, hidden), BF16),
        pltpu.VMEM((2, f_x, hidden), BF16),
        pltpu.VMEM((2, z_n, piece, hidden), BF16),
        pltpu.VMEM((2, y_n, piece, hidden), BF16),
        pltpu.VMEM((2, width, hidden), BF16),
        pltpu.VMEM((2, 8, hidden), F32),
        pltpu.VMEM((X, 8, hidden), F32),
        pltpu.VMEM((z_n, 8, hidden), F32),
        pltpu.VMEM((y_n, 8, hidden), F32),
        pltpu.VMEM((8, LANES), jnp.int32),
        pltpu.SMEM((8, LANES), jnp.int32),
        pltpu.SemaphoreType.DMA((2,)),
        pltpu.SemaphoreType.DMA((copies,)),
        pltpu.SemaphoreType.DMA((copies,)),
    ]
    node_out, feat_grad, self_grad, neigh_grad, offset_grad = pl.pallas_call(
        functools.partial(kernel, rows, cols, slots, scale),
        out_shape=(
            jax.ShapeDtypeStruct((nodes_dev, hidden), BF16),
            jax.ShapeDtypeStruct((nodes_dev, width), BF16),
            jax.ShapeDtypeStruct((width, hidden), BF16),
            jax.ShapeDtypeStruct((width, hidden), BF16),
            jax.ShapeDtypeStruct((1, hidden), F32),
        ),
        in_specs=[vmem, vmem, pl.BlockSpec(memory_space=pl.ANY), vmem,
                  pl.BlockSpec(memory_space=pltpu.SMEM), vmem, vmem, vmem, vmem],
        out_specs=[vmem] * 5,
        scratch_shapes=scratch,
        compiler_params=pltpu.CompilerParams(
            collective_id=0, has_side_effects=True, vmem_limit_bytes=48 * 1024 * 1024
        ),
    )(
        features, degree.reshape(1, nodes_dev), blocks.reshape(slots, side, side),
        coords.reshape(1, slots), counts, w_self, w_neigh, offset.reshape(1, hidden), cotangent,
    )
    return node_out, feat_grad, self_grad, neigh_grad, offset_grad.reshape(hidden)


def solution(mesh):
    return jax.shard_map(
        functools.partial(run, mesh.shape["row"], mesh.shape["col"]),
        mesh=mesh,
        in_specs=(
            P(("row", "col"), None),
            P(("row", "col")),
            P("row", "col", None, None, None),
            P("row", "col", None),
            P("row", "col"),
            P(),
            P(),
            P(),
            P(("row", "col"), None),
        ),
        out_specs=(P(("row", "col"), None), P(("row", "col"), None), P(), P(), P()),
        check_vma=False,
    )
```

```python
import functools
import math

import jax
import jax.numpy as jnp
from jax import lax
from jax.experimental import pallas as pl
from jax.experimental.pallas import tpu as pltpu
from jax.sharding import PartitionSpec as P

MESH = pl.DeviceIdType.MESH
BF16 = jnp.bfloat16
F32 = jnp.float32
X = 4
LANES = 128
BIG = 1 << 20


def spread_t(row):
    return jnp.broadcast_to(row, (LANES, LANES)).T


def slot_tables(group, other, used, slots):
    lane = lax.broadcasted_iota(jnp.int32, (LANES, LANES), 1)
    sub = lax.broadcasted_iota(jnp.int32, (LANES, LANES), 0)
    key = jnp.where(used > 0, group * LANES + lane[:1], BIG + lane[:1])
    key_r = jnp.broadcast_to(key, (LANES, LANES))
    key_c = spread_t(key)
    grp_r = jnp.broadcast_to(group, (LANES, LANES))
    grp_c = spread_t(group)
    used_c = spread_t(used)
    other_c = spread_t(other)
    less = jnp.where(key_r < key_c, 1, 0)
    rank = jnp.sum(less, axis=1, keepdims=True)
    same = jnp.where(grp_r == grp_c, less, 0)
    keep = jnp.minimum(jnp.sum(same, axis=1, keepdims=True), 1)
    hot = rank == lane
    order = jnp.sum(jnp.where(hot, sub, 0), axis=0, keepdims=True)
    there = jnp.sum(jnp.where(hot, other_c, 0), axis=0, keepdims=True)
    keeps = jnp.sum(jnp.where(hot, keep, 0), axis=0, keepdims=True)
    upto = jnp.sum(jnp.where(grp_c <= lane, used_c, 0), axis=0, keepdims=True)
    here = jnp.sum(jnp.where(grp_c == lane, used_c, 0), axis=0, keepdims=True)
    last = jnp.where(here > 0, upto - 1, slots)
    return [order, there, keeps, last]


def kernel(
    rows, cols, slots, scale,
    feat_hbm, deg_hbm, blocks_hbm, coords_hbm, counts_hbm, ws_hbm, wn_hbm, off_hbm, cot_hbm,
    node_hbm, fgrad_hbm, sgrad_hbm, ngrad_hbm, ograd_hbm,
    node_ref, fgrad_ref, ograd_ref, feats_t,
    feat_ref, deg_ref, tiles, coords_ref, counts_ref, ws_ref, wn_ref, off_ref, cot_ref,
    panel, sums, part, core_in, flow_out, flow_in, far_out, far_in, yh_out, yh_in, bands, back,
    ring_in, line_out, line_in, own_pre, fsum,
    e1_out, e1_in, e2_out, e2_in, e3_out, e3_in, e4, egather, o1, o2, o3, o4,
    table_v, table_s, copy_sem, out_sem, send_sem, recv_sem,
):
    yl_n = rows // X
    z_n = cols // 4
    row = lax.axis_index("row")
    col = lax.axis_index("col")
    x = lax.rem(row, X)
    yl = row // X
    z = col // 4
    yh = lax.rem(col // 2, 2)
    c = lax.rem(col, 2)
    src_n = rows
    dest_n = cols

    def at(yl_=None, x_=None, z_=None, yh_=None, c_=None):
        yl_ = yl if yl_ is None else yl_
        x_ = x if x_ is None else x_
        z_ = z if z_ is None else z_
        yh_ = yh if yh_ is None else yh_
        c_ = c if c_ is None else c_
        return (yl_ * X + x_, z_ * 4 + yh_ * 2 + c_)

    def turn(i, d, n):
        return lax.rem(i + (d % n), n)

    y_n = 2 * yl_n
    y = yh * yl_n + yl

    def at_y(y_):
        return at(yl_=lax.rem(y_, yl_n), yh_=y_ // yl_n)

    x_peers = [at(x_=turn(x, d, X)) for d in range(1, X)]
    z_peers = [at(z_=turn(z, d, z_n)) for d in range(1, z_n)]
    y_peers = [at_y(turn(y, d, y_n)) for d in range(1, y_n)]
    core_peer = at(c_=1 - c)
    peers = x_peers + z_peers + y_peers + [core_peer]

    near_first = sorted(range(1, yl_n), key=lambda d: min(d, yl_n - d))
    issued = []

    def put(src, dst, device):
        i = len(issued)
        copy = pltpu.make_async_remote_copy(
            src_ref=src, dst_ref=dst, send_sem=send_sem.at[i], recv_sem=recv_sem.at[i],
            device_id=device, device_id_type=MESH,
        )
        copy.start()
        issued.append(copy)
        return copy

    saved = []

    def save(src, dst):
        copy = pltpu.make_async_copy(src, dst, out_sem.at[len(saved)])
        copy.start()
        saved.append(copy)

    def dot(a, b):
        return jnp.dot(a, b, preferred_element_type=F32)

    def dot_t(a, b):
        return lax.dot_general(a, b, (((0,), (0,)), ((), ())), preferred_element_type=F32)

    def dot_nt(a, b):
        return lax.dot_general(a, b, (((1,), (1,)), ((), ())), preferred_element_type=F32)

    loads = {}
    for i, (name, there, here) in enumerate((
        ("feat", feat_hbm, feat_ref), ("wn", wn_hbm, wn_ref), ("coords", coords_hbm, coords_ref),
        ("counts", counts_hbm, counts_ref), ("ws", ws_hbm, ws_ref), ("off", off_hbm, off_ref),
        ("tiles", blocks_hbm, tiles), ("deg", deg_hbm, deg_ref), ("cot", cot_hbm, cot_ref),
    )):
        loads[name] = pltpu.make_async_copy(there, here, copy_sem.at[i])
        loads[name].start()
    barrier = pltpu.get_barrier_semaphore()
    for peer in peers:
        pl.semaphore_signal(barrier, inc=1, device_id=peer, device_id_type=MESH)
    loads["feat"].wait()
    loads["wn"].wait()
    panel[x * yl_n + yl] = dot(feat_ref[...], wn_ref[...]).astype(BF16)
    pl.semaphore_wait(barrier, len(peers))

    mine = panel.at[x * yl_n + yl]
    a_line = {d: put(mine, mine, at(yl_=turn(yl, d, yl_n))) for d in near_first}
    a_ring = [put(mine, mine, peer) for peer in x_peers]

    loads["coords"].wait()
    loads["counts"].wait()
    table_v[...] = jnp.zeros_like(table_v)
    table_v[0:1, 0:slots] = coords_ref[...]
    code = table_v[0:1, :]
    lane = lax.broadcasted_iota(jnp.int32, (1, LANES), 1)
    used = jnp.where(lane < counts_ref[0, 0], 1, 0)
    src_bits = (src_n - 1).bit_length()
    dest = lax.shift_right_logical(code, src_bits)
    src = lax.bitwise_and(code, src_n - 1)
    dest_q = lax.bitwise_and(dest, 1) * (dest_n // 2) + lax.shift_right_logical(dest, 1)
    src_q = lax.bitwise_and(src, X - 1) * yl_n + lax.shift_right_logical(src, 2)
    lines = slot_tables(dest_q, src_q, used, slots)
    lines += slot_tables(src_q, dest_q, used, slots)
    for i, line in enumerate(lines):
        table_v[i:i + 1, :] = line
    table_copy = pltpu.make_async_copy(table_v, table_s, copy_sem.at[9])
    table_copy.start()

    for d in near_first:
        a_line[d].wait_recv()
        ref = panel.at[x * yl_n + turn(yl, -d, yl_n)]
        a_ring += [put(ref, ref, peer) for peer in x_peers]
    loads["ws"].wait()
    loads["off"].wait()
    off = jnp.concatenate([off_ref[i:i + 1, :] for i in range(off_ref.shape[0])], axis=1)
    own_pre[...] = dot(feat_ref[...], ws_ref[...]) + off.astype(F32)
    sums[slots] = jnp.zeros_like(sums[slots])
    feats_t[x * yl_n + yl] = feat_ref[...].T
    loads["tiles"].wait()
    loads["deg"].wait()
    loads["cot"].wait()
    table_copy.wait()
    for copy in a_ring:
        copy.wait_recv()

    mine_t = feats_t.at[x * yl_n + yl]
    f_line = {d: put(mine_t, mine_t, at(yl_=turn(yl, d, yl_n))) for d in near_first}
    f_ring = [put(mine_t, mine_t, peer) for peer in x_peers]

    def feats_on(d):
        f_line[d].wait_recv()
        ref = feats_t.at[x * yl_n + turn(yl, -d, yl_n)]
        f_ring.extend([put(ref, ref, peer) for peer in x_peers])

    def products(line, matrix, operand):
        def step(k, total):
            tile = tiles[table_s[line, k]]
            rows_in = operand[table_s[line + 1, k]]
            total = total * table_s[line + 2, k].astype(F32) + matrix(tile, rows_in)
            sums[k] = total.astype(BF16)
            return total
        lax.fori_loop(0, slots, step, jnp.zeros(sums.shape[1:], F32), unroll=4)

    products(0, dot, panel)

    def chunk(d, r):
        return turn(z, d, z_n) * 2 + (yh if r == 0 else 1 - yh)

    core_copy = {}
    for r in (1, 0):
        for d in (4, 3, -3, 2, -2, 1, -1, 0):
            q = chunk(d, r)
            part[(1 - c) * (dest_n // 2) + q] = sums[table_s[3, (1 - c) * (dest_n // 2) + q]]
            core_copy[(d, r)] = put(part.at[(1 - c) * (dest_n // 2) + q], core_in.at[q], core_peer)

    def take(q, _):
        part[c * (dest_n // 2) + q] = sums[table_s[3, c * (dest_n // 2) + q]]
        return 0
    lax.fori_loop(0, dest_n // 2, take, 0)

    def own2(d, r):
        core_copy[(d, r)].wait_recv()
        q = chunk(d, r)
        return part[c * (dest_n // 2) + q].astype(F32) + core_in[q].astype(F32)

    def z_at(d):
        return at(z_=turn(z, d, z_n))

    mid = part.shape[1] // 2
    got = {}

    def far_dest(r):
        value = own2(4, r).astype(BF16)
        far_out[r] = value
        for i, way in enumerate((1, -1)):
            part_ref = pl.ds(i * mid, mid)
            got[(r, 4 * way)] = put(far_out.at[r, part_ref], far_in.at[r, part_ref], z_at(2 * way))
        for way in (1, -1):
            send(r, 3 * way, own2(3 * way, r), z_at(way))

    def send(r, d, value, device):
        i = r * 6 + {3: 0, -3: 1, 2: 2, -2: 3, 1: 4, -1: 5}[d]
        flow_out[i] = value.astype(BF16)
        got[(r, d)] = put(flow_out.at[i], flow_in.at[i], device)

    def came(r, d):
        got[(r, d)].wait_recv()
        return flow_in[r * 6 + {3: 0, -3: 1, 2: 2, -2: 3, 1: 4, -1: 5}[d]].astype(F32)

    def near_dest(r):
        for way in (1, -1):
            send(r, way, own2(way, r), z_at(way))

    def merged(r):
        for i, way in enumerate((1, -1)):
            value = own2(2 * way, r) + came(r, 3 * way)
            got[(r, 4 * way)].wait_recv()
            far = far_in[r, i * mid:(i + 1) * mid].astype(F32)
            if i == 0:
                value = jnp.concatenate([value[:mid] + far, value[mid:]], axis=0)
            else:
                value = jnp.concatenate([value[:mid], value[mid:] + far], axis=0)
            send(r, 2 * way, value, z_at(2 * way))

    def arrived(r):
        value = own2(0, r)
        for d in (1, -1, 2, -2):
            value = value + came(r, d)
        return value

    far_dest(1)
    near_dest(1)
    far_dest(0)
    merged(1)
    near_dest(0)
    merged(0)
    for d in near_first:
        feats_on(d)
    yh_out[...] = arrived(1).astype(BF16)
    yh_copy = put(yh_out, yh_in, at(yh_=1 - yh))
    mine_sum = arrived(0)
    yh_copy.wait_recv()
    aggregate = mine_sum + yh_in[...].astype(F32)

    deg = jnp.broadcast_to(deg_ref[...].astype(F32), (LANES, LANES)).T
    deg = jnp.concatenate([deg] * (aggregate.shape[1] // LANES), axis=1)
    preact = own_pre[...] + aggregate / deg
    sig = jax.nn.sigmoid(preact)
    dpre = cot_ref[...].astype(F32) * sig * (1.0 + preact * (1.0 - sig))
    dpre_b = dpre.astype(BF16)
    own_band = c * (dest_n // 2) + z * 2 + yh
    bands[own_band] = (dpre / deg).astype(BF16)

    def band(d, r):
        return bands.at[c * (dest_n // 2) + chunk(d, r)]

    to_core = []
    hop = {}

    def core_too(d, r):
        to_core.append(put(band(d, r), band(d, r), core_peer))

    def spread(r):
        for d in (2, -2, 1, -1):
            hop[(r, d)] = put(band(0, r), band(0, r), z_at(d))
        core_too(0, r)

    def onward(r):
        for i, way in enumerate((1, -1)):
            hop[(r, 2 * way)].wait_recv()
            ref = band(-2 * way, r)
            part_ref = ref.at[pl.ds(i * mid, mid)]
            hop[(r, 4 * way)] = put(part_ref, part_ref, z_at(2 * way))
            hop[(r, 3 * way)] = put(ref, ref, z_at(way))
            core_too(-2 * way, r)
        for way in (1, -1):
            hop[(r, way)].wait_recv()
            core_too(-way, r)

    def settle(r):
        for way in (1, -1):
            hop[(r, 3 * way)].wait_recv()
            core_too(-3 * way, r)
        for way in (1, -1):
            hop[(r, 4 * way)].wait_recv()
        core_too(4, r)

    c_yh = put(band(0, 0), band(0, 0), at(yh_=1 - yh))
    spread(0)
    node_ref[...] = (preact * sig).astype(BF16)
    save(node_ref, node_hbm)

    piece = feat_ref.shape[1] // (2 * X * z_n)
    f_half = feat_ref.shape[1] // 2
    f_x = f_half // X

    def all_reduce(i, value, side):
        if value is not None:
            fsum[i] = value
        e1_out[i] = fsum[i, pl.ds((1 - c) * f_half, f_half)].astype(BF16)
        copy = put(e1_out.at[i], e1_in.at[i], core_peer)
        if side is not None:
            o1[c] = side
            o_copies = [put(o1.at[c], o1.at[c], core_peer)]
        yield
        copy.wait_recv()
        fsum[i, 0:f_half] = fsum[i, pl.ds(c * f_half, f_half)] + e1_in[i].astype(F32)
        e2_out[i] = fsum[i, 0:f_half].astype(BF16)
        copies = []
        for d in range(1, X):
            there = turn(x, d, X)
            copies.append(put(e2_out.at[i, pl.ds(there * f_x, f_x)], e2_in.at[i, d], at(x_=there)))
        if side is not None:
            for o_copy in o_copies:
                o_copy.wait_recv()
            o2[x] = jnp.sum(o1[...], axis=0)
            o_copies = [put(o2.at[x], o2.at[x], peer) for peer in x_peers]
        yield
        total = fsum[i, pl.ds(x * f_x, f_x)]
        for d in range(1, X):
            copies[d - 1].wait_recv()
            total = total + e2_in[i, d].astype(F32)
        fsum[i, 0:f_x] = total
        e3_out[i] = total.astype(BF16)
        copies = []
        for d in range(1, z_n):
            there = turn(z, d, z_n)
            copies.append(put(e3_out.at[i, pl.ds(there * piece, piece)], e3_in.at[i, d], at(z_=there)))
        if side is not None:
            for o_copy in o_copies:
                o_copy.wait_recv()
            o3[z] = jnp.sum(o2[...], axis=0)
            o_copies = [put(o3.at[z], o3.at[z], peer) for peer in z_peers]
        yield
        total = fsum[i, pl.ds(z * piece, piece)]
        for d in range(1, z_n):
            copies[d - 1].wait_recv()
            total = total + e3_in[i, d].astype(F32)
        e4[i, y] = total.astype(BF16)
        copies = [put(e4.at[i, y], e4.at[i, y], peer) for peer in y_peers]
        if side is not None:
            for o_copy in o_copies:
                o_copy.wait_recv()
            o4[y] = jnp.sum(o3[...], axis=0)
            o_copies = [put(o4.at[y], o4.at[y], peer) for peer in y_peers]
        yield
        for copy in copies:
            copy.wait_recv()
        total = e4[i, 0].astype(F32)
        for there in range(1, y_n):
            total = total + e4[i, there].astype(F32)
        start = c * f_half + x * f_x + z * piece
        egather[i, pl.ds(start, piece)] = (total * scale).astype(BF16)
        ref = egather.at[i, pl.ds(start, piece)]
        copies = [put(ref, ref, peer) for peer in z_peers]
        if side is not None:
            for o_copy in o_copies:
                o_copy.wait_recv()
            ograd_ref[...] = (jnp.sum(o4[...], axis=0) * scale)[0:1]
            save(ograd_ref, ograd_hbm)
        yield
        for copy in copies:
            copy.wait_recv()
        ref = egather.at[i, pl.ds(c * f_half + x * f_x, f_x)]
        copies = [put(ref, ref, peer) for peer in x_peers]
        yield
        for copy in copies:
            copy.wait_recv()
        ref = egather.at[i, pl.ds(c * f_half, f_half)]
        copy = put(ref, ref, core_peer)
        yield
        copy.wait_recv()
        save(egather.at[i], sgrad_hbm if i == 0 else ngrad_hbm)

    side = jnp.broadcast_to(jnp.sum(dpre, axis=0, keepdims=True), o1.shape[1:])
    self_steps = all_reduce(0, dot(feats_t[x * yl_n + yl], dpre_b), side)
    next(self_steps)

    own_pre[...] = dpre
    onward(0)
    c_yh.wait_recv()
    spread(1)
    settle(0)
    onward(1)
    next(self_steps)
    settle(1)
    for copy in to_core:
        copy.wait_recv()

    products(4, dot_t, bands)

    def take_back(q, _):
        back[q] = sums[table_s[7, q]]
        return 0
    lax.fori_loop(0, src_n, take_back, 0)

    def back_at(dx, d):
        return turn(x, dx, X) * yl_n + turn(yl, d, yl_n)

    for copy in f_ring:
        copy.wait_recv()

    def share(m, _):
        at_m = pl.ds(pl.multiple_of(m * LANES, LANES), LANES)
        total = jnp.zeros((LANES, back.shape[2]), F32)
        for q in range(0, src_n, 2):
            left_in = jnp.concatenate([feats_t[q, at_m], feats_t[q + 1, at_m]], axis=1)
            right_in = back[q:q + 2].reshape(2 * back.shape[1], back.shape[2])
            total = total + dot(left_in, right_in)
        fsum[1, at_m] = total
        return 0
    lax.fori_loop(0, feats_t.shape[1] // LANES, share, 0)

    neigh_steps = all_reduce(1, None, None)
    next(neigh_steps)
    next(self_steps)
    next(neigh_steps)

    order = near_first[::-1] + [0]
    ring = {}
    for d in order:
        for dx in range(1, X):
            ring[(dx, d)] = put(back.at[back_at(dx, d)], ring_in.at[dx - 1, d], x_peers[dx - 1])
    next(self_steps)
    next(neigh_steps)
    next(self_steps)
    next(neigh_steps)
    y_copy = {}
    for d in order:
        value = back[back_at(0, d)].astype(F32)
        for dx in range(1, X):
            ring[(dx, d)].wait_recv()
            value = value + ring_in[dx - 1, d].astype(F32)
        if d > 0:
            line_out[d] = value.astype(BF16)
            y_copy[d] = put(line_out.at[d], line_in.at[d], at(yl_=turn(yl, d, yl_n)))
        else:
            dprop = value
    next(self_steps)
    next(neigh_steps)
    for d in range(1, yl_n):
        y_copy[d].wait_recv()
        dprop = dprop + line_in[d].astype(F32)
    fgrad_ref[...] = (
        dot_nt(own_pre[...].astype(BF16), ws_ref[...]) + dot_nt(dprop.astype(BF16), wn_ref[...])
    ).astype(BF16)
    save(fgrad_ref, fgrad_hbm)
    next(self_steps)
    next(neigh_steps)
    next(self_steps, None)
    next(neigh_steps)
    next(neigh_steps, None)
    for copy in issued:
        copy.wait_send()
    for copy in saved:
        copy.wait()


def hand_on(*refs):
    count = (len(refs) - 2) // 3
    there, here, held = refs[:count], refs[count:2 * count], refs[2 * count:3 * count]
    sem_in, sem_out = refs[-2:]
    fetch = [pltpu.make_async_copy(there[i], held[i], sem_in.at[i]) for i in range(count)]
    store = [pltpu.make_async_copy(held[i], here[i], sem_out.at[i]) for i in range(count)]
    for copy in fetch:
        copy.start()
    for i in range(count):
        fetch[i].wait()
        store[i].start()
    for copy in store:
        copy.wait()


def run(rows, cols, features, degree, blocks, coords, counts, w_self, w_neigh, offset, cotangent):
    nodes_dev, hidden = cotangent.shape
    width = features.shape[1]
    slots, side = blocks.shape[2], blocks.shape[3]
    z_n, yl_n = cols // 4, rows // X
    y_n = 2 * yl_n
    f_half = width // 2
    f_x = f_half // X
    piece = f_x // z_n
    scale = 1.0 / math.sqrt(nodes_dev * rows * cols)
    hbm = pl.BlockSpec(memory_space=pl.ANY)
    block = (side, hidden)
    copies = 400
    scratch = [
        pltpu.VMEM((nodes_dev, hidden), BF16),
        pltpu.VMEM((nodes_dev, width), BF16),
        pltpu.VMEM((1, hidden), F32),
        pltpu.VMEM((rows, width, nodes_dev), BF16),
        pltpu.VMEM((nodes_dev, width), BF16),
        pltpu.VMEM((1, nodes_dev), jnp.int32),
        pltpu.VMEM((slots, side, side), BF16),
        pltpu.VMEM((1, slots), jnp.int32),
        pltpu.SMEM((1, 1), jnp.int32),
        pltpu.VMEM((width, hidden), BF16),
        pltpu.VMEM((width, hidden), BF16),
        pltpu.VMEM((hidden // LANES, LANES), BF16),
        pltpu.VMEM((nodes_dev, hidden), BF16),
        pltpu.VMEM((rows,) + block, BF16),
        pltpu.VMEM((slots + 1,) + block, BF16),
        pltpu.VMEM((cols,) + block, BF16),
        pltpu.VMEM((cols // 2,) + block, BF16),
        pltpu.VMEM((12,) + block, BF16),
        pltpu.VMEM((12,) + block, BF16),
        pltpu.VMEM((2,) + block, BF16),
        pltpu.VMEM((2,) + block, BF16),
        pltpu.VMEM(block, BF16),
        pltpu.VMEM(block, BF16),
        pltpu.VMEM((cols,) + block, BF16),
        pltpu.VMEM((rows,) + block, BF16),
        pltpu.VMEM((3, yl_n) + block, BF16),
        pltpu.VMEM((yl_n,) + block, BF16),
        pltpu.VMEM((yl_n,) + block, BF16),
        pltpu.VMEM((nodes_dev, hidden), F32),
        pltpu.VMEM((2, width, hidden), F32),
        pltpu.VMEM((2, f_half, hidden), BF16),
        pltpu.VMEM((2, f_half, hidden), BF16),
        pltpu.VMEM((2, f_half, hidden), BF16),
        pltpu.VMEM((2, X, f_x, hidden), BF16),
        pltpu.VMEM((2, f_x, hidden), BF16),
        pltpu.VMEM((2, z_n, piece, hidden), BF16),
        pltpu.VMEM((2, y_n, piece, hidden), BF16),
        pltpu.VMEM((2, width, hidden), BF16),
        pltpu.VMEM((2, 8, hidden), F32),
        pltpu.VMEM((X, 8, hidden), F32),
        pltpu.VMEM((z_n, 8, hidden), F32),
        pltpu.VMEM((y_n, 8, hidden), F32),
        pltpu.VMEM((8, LANES), jnp.int32),
        pltpu.SMEM((8, LANES), jnp.int32),
        pltpu.SemaphoreType.DMA((10,)),
        pltpu.SemaphoreType.DMA((5,)),
        pltpu.SemaphoreType.DMA((copies,)),
        pltpu.SemaphoreType.DMA((copies,)),
    ]
    shapes = (
            jax.ShapeDtypeStruct((nodes_dev, hidden), BF16),
            jax.ShapeDtypeStruct((nodes_dev, width), BF16),
            jax.ShapeDtypeStruct((width, hidden), BF16),
            jax.ShapeDtypeStruct((width, hidden), BF16),
            jax.ShapeDtypeStruct((1, hidden), F32),
        )
    results = pl.pallas_call(
        functools.partial(kernel, rows, cols, slots, scale),
        out_shape=shapes,
        in_specs=[hbm] * 9,
        out_specs=[hbm] * 5,
        scratch_shapes=scratch,
        compiler_params=pltpu.CompilerParams(
            collective_id=0, has_side_effects=True, vmem_limit_bytes=60 * 1024 * 1024
        ),
    )(
        features, degree.reshape(1, nodes_dev), blocks.reshape(slots, side, side),
        coords.reshape(1, slots), counts, w_self, w_neigh, offset.reshape(hidden // LANES, LANES), cotangent,
    )
    node_out, feat_grad, self_grad, neigh_grad, offset_grad = pl.pallas_call(
        hand_on,
        out_shape=shapes,
        in_specs=[hbm] * 5,
        out_specs=[hbm] * 5,
        scratch_shapes=[pltpu.VMEM(held.shape, held.dtype) for held in shapes]
        + [pltpu.SemaphoreType.DMA((5,)), pltpu.SemaphoreType.DMA((5,))],
        compiler_params=pltpu.CompilerParams(vmem_limit_bytes=60 * 1024 * 1024),
    )(*results)
    return node_out, feat_grad, self_grad, neigh_grad, offset_grad.reshape(hidden)


def solution(mesh):
    return jax.shard_map(
        functools.partial(run, mesh.shape["row"], mesh.shape["col"]),
        mesh=mesh,
        in_specs=(
            P(("row", "col"), None),
            P(("row", "col")),
            P("row", "col", None, None, None),
            P("row", "col", None),
            P("row", "col"),
            P(),
            P(),
            P(),
            P(("row", "col"), None),
        ),
        out_specs=(P(("row", "col"), None), P(("row", "col"), None), P(), P(), P()),
        check_vma=False,
    )
```

```python
import functools
import math

import jax
import jax.numpy as jnp
from jax import lax
from jax.experimental import pallas as pl
from jax.experimental.pallas import tpu as pltpu
from jax.sharding import PartitionSpec as P

MESH = pl.DeviceIdType.MESH
BF16 = jnp.bfloat16
F32 = jnp.float32
X = 4
LANES = 128
SUM_ORDER = (4, 3, -3, 1, -1, 2, -2, 0)
HAND_ORDER = (0, 2, -2, 1, -1, 3, -3, 4)
BIG = 1 << 20
SEND_POOL = 48


def spread_t(row):
    return jnp.broadcast_to(row, (LANES, LANES)).T


def slot_tables(group, other, used, slots):
    lane = lax.broadcasted_iota(jnp.int32, (LANES, LANES), 1)
    sub = lax.broadcasted_iota(jnp.int32, (LANES, LANES), 0)
    key = jnp.where(used > 0, group * LANES + lane[:1], BIG + lane[:1])
    key_r = jnp.broadcast_to(key, (LANES, LANES))
    key_c = spread_t(key)
    grp_r = jnp.broadcast_to(group, (LANES, LANES))
    grp_c = spread_t(group)
    used_c = spread_t(used)
    other_c = spread_t(other)
    less = jnp.where(key_r < key_c, 1, 0)
    rank = jnp.sum(less, axis=1, keepdims=True)
    same = jnp.where(grp_r == grp_c, less, 0)
    keep = jnp.minimum(jnp.sum(same, axis=1, keepdims=True), 1)
    hot = rank == lane
    order = jnp.sum(jnp.where(hot, sub, 0), axis=0, keepdims=True)
    there = jnp.sum(jnp.where(hot, other_c, 0), axis=0, keepdims=True)
    keeps = jnp.sum(jnp.where(hot, keep, 0), axis=0, keepdims=True)
    upto = jnp.sum(jnp.where(grp_c <= lane, used_c, 0), axis=0, keepdims=True)
    here = jnp.sum(jnp.where(grp_c == lane, used_c, 0), axis=0, keepdims=True)
    last = jnp.where(here > 0, upto - 1, slots)
    return [order, there, keeps, last]


def kernel(
    rows, cols, slots, scale,
    feat_hbm, deg_hbm, blocks_hbm, coords_hbm, counts_hbm, ws_hbm, wn_hbm, off_hbm, cot_hbm,
    node_hbm, fgrad_hbm, sgrad_hbm, ngrad_hbm, ograd_hbm,
    node_ref, fgrad_ref, ograd_ref, feats_t, deg_t,
    feat_ref, deg_ref, tiles, coords_ref, counts_ref, ws_ref, wn_ref, off_ref, cot_ref,
    panel, sums, part, core_in, flow_out, flow_in, far_out, far_in, yh_out, yh_in, bands, back,
    ring_in, line_out, line_in, own_pre, fsum,
    e1_out, e1_in, e2_out, e2_in, e3_out, e3_in, e4, egather, o1, o2, o3, o4,
    table_v, table_s, copy_sem, out_sem, send_sem, recv_sem,
):
    yl_n = rows // X
    z_n = cols // 4
    row = lax.axis_index("row")
    col = lax.axis_index("col")
    x = lax.rem(row, X)
    yl = row // X
    z = col // 4
    yh = lax.rem(col // 2, 2)
    c = lax.rem(col, 2)
    src_n = rows
    dest_n = cols

    def at(yl_=None, x_=None, z_=None, yh_=None, c_=None):
        yl_ = yl if yl_ is None else yl_
        x_ = x if x_ is None else x_
        z_ = z if z_ is None else z_
        yh_ = yh if yh_ is None else yh_
        c_ = c if c_ is None else c_
        return (yl_ * X + x_, z_ * 4 + yh_ * 2 + c_)

    def turn(i, d, n):
        return lax.rem(i + (d % n), n)

    y_n = 2 * yl_n
    y = yh * yl_n + yl

    def at_y(y_):
        return at(yl_=lax.rem(y_, yl_n), yh_=y_ // yl_n)

    def far_first(n):
        return sorted(range(1, n), key=lambda d: -min(d, n - d))

    x_peers = [at(x_=turn(x, d, X)) for d in far_first(X)]
    z_peers = [at(z_=turn(z, d, z_n)) for d in far_first(z_n)]
    y_peers = [at_y(turn(y, d, y_n)) for d in far_first(y_n)]
    core_peer = at(c_=1 - c)
    across = [at(z_=turn(z, d, z_n), yh_=1 - yh) for d in (2, -2)]
    peers = x_peers + z_peers + y_peers + across + [core_peer]

    away = range(1, yl_n)

    def mate(d):
        if d == 1:
            return yl + 1 - 2 * lax.rem(yl, 2)
        if d == 2:
            return lax.rem(yl + 2, 4)
        return 3 - yl if d == 3 else yl

    issued = []
    drained = [0]

    def drain(keep):
        while drained[0] < len(issued) - keep:
            issued[drained[0]].wait_send()
            drained[0] += 1

    def next_slot(message):
        issued.append(message)
        drain(SEND_POOL)
        i = len(issued) - 1
        return send_sem.at[i % SEND_POOL], recv_sem.at[i]

    class Bundle:
        def __init__(self, span):
            self.span = span
            self.send, self.recv = next_slot(self)

        def put(self, src, dst, device):
            pltpu.make_async_remote_copy(
                src_ref=src, dst_ref=dst, send_sem=self.send, recv_sem=self.recv,
                device_id=device, device_id_type=MESH,
            ).start()

        def wait_recv(self):
            pltpu.make_async_copy(self.span, self.span, self.recv).wait()

        def wait_send(self):
            pltpu.make_async_copy(self.span, self.span, self.send).wait()

    def put(src, dst, device):
        message = Bundle(dst)
        message.put(src, dst, device)
        return message

    def put_all(span, ref, devices):
        bundle = Bundle(span)
        for device in devices:
            bundle.put(ref, ref, device)
        return bundle

    saved = []

    def save(src, dst):
        copy = pltpu.make_async_copy(src, dst, out_sem.at[len(saved)])
        copy.start()
        saved.append(copy)

    def dot(a, b):
        return jnp.dot(a, b, preferred_element_type=F32)

    def dot_t(a, b):
        return lax.dot_general(a, b, (((0,), (0,)), ((), ())), preferred_element_type=F32)

    def dot_nt(a, b):
        return lax.dot_general(a, b, (((1,), (1,)), ((), ())), preferred_element_type=F32)

    loads = {}
    for i, (name, there, here) in enumerate((
        ("feat", feat_hbm, feat_ref), ("wn", wn_hbm, wn_ref), ("coords", coords_hbm, coords_ref),
        ("counts", counts_hbm, counts_ref), ("ws", ws_hbm, ws_ref), ("off", off_hbm, off_ref),
        ("tiles", blocks_hbm, tiles), ("deg", deg_hbm, deg_ref), ("cot", cot_hbm, cot_ref),
    )):
        loads[name] = pltpu.make_async_copy(there, here, copy_sem.at[i])
        loads[name].start()
    barrier = pltpu.get_barrier_semaphore()
    for peer in peers:
        pl.semaphore_signal(barrier, inc=1, device_id=peer, device_id_type=MESH)
    loads["feat"].wait()
    loads["wn"].wait()
    panel[x * yl_n + yl] = dot(feat_ref[...], wn_ref[...]).astype(BF16)
    pl.semaphore_wait(barrier, len(peers))

    mine = panel.at[x * yl_n + yl]
    a_line = {d: put(mine, mine, at(yl_=mate(d))) for d in away}
    a_ring = put_all(panel.at[pl.ds(0, (X - 1) * yl_n)], mine, x_peers)

    loads["coords"].wait()
    loads["counts"].wait()
    table_v[...] = jnp.zeros_like(table_v)
    table_v[0:1, 0:slots] = coords_ref[...]
    code = table_v[0:1, :]
    lane = lax.broadcasted_iota(jnp.int32, (1, LANES), 1)
    used = jnp.where(lane < counts_ref[0, 0], 1, 0)
    src_bits = (src_n - 1).bit_length()
    dest = lax.shift_right_logical(code, src_bits)
    src = lax.bitwise_and(code, src_n - 1)
    dest_q = lax.bitwise_and(dest, 1) * (dest_n // 2) + lax.shift_right_logical(dest, 1)
    src_q = lax.bitwise_and(src, X - 1) * yl_n + lax.shift_right_logical(src, 2)
    lines = slot_tables(dest_q, src_q, used, slots)
    away_z = lax.rem(lax.shift_right_logical(dest, 2) - z + z_n, z_n)
    place = jnp.zeros_like(away_z)
    for i, d in enumerate(HAND_ORDER):
        place = jnp.where(away_z == d % z_n, i, place)
    other_yh = jnp.where(lax.bitwise_and(lax.shift_right_logical(dest, 1), 1) == yh, 0, z_n)
    hand_q = lax.bitwise_and(dest, 1) * (dest_n // 2) + other_yh + place
    lines += slot_tables(src_q, hand_q, used, slots)
    for i, line in enumerate(lines):
        table_v[i:i + 1, :] = line
    table_copy = pltpu.make_async_copy(table_v, table_s, copy_sem.at[9])
    table_copy.start()

    for d in away:
        a_line[d].wait_recv()
        ref = panel.at[x * yl_n + mate(d)]
        for peer in x_peers:
            a_ring.put(ref, ref, peer)
    feats_t[x * yl_n + yl] = feat_ref[...].T
    mine_t = feats_t.at[x * yl_n + yl]
    f_line = {d: put(mine_t, mine_t, at(yl_=mate(d))) for d in away}
    loads["ws"].wait()
    loads["off"].wait()
    off = jnp.concatenate([off_ref[i:i + 1, :] for i in range(off_ref.shape[0])], axis=1)
    own_pre[...] = dot(feat_ref[...], ws_ref[...]) + off.astype(F32)
    sums[slots] = jnp.zeros_like(sums[slots])
    loads["tiles"].wait()
    loads["deg"].wait()
    loads["cot"].wait()
    deg_t[...] = spread_t(deg_ref[...].astype(F32))
    table_copy.wait()
    a_ring.wait_recv()

    f_ring = put_all(feats_t.at[pl.ds(0, (X - 1) * yl_n)], mine_t, x_peers)

    def feats_on(d):
        f_line[d].wait_recv()
        ref = feats_t.at[x * yl_n + mate(d)]
        for peer in x_peers:
            f_ring.put(ref, ref, peer)

    def products(line, matrix, operand):
        def step(k, total):
            tile = tiles[table_s[line, k]]
            rows_in = operand[table_s[line + 1, k]]
            total = total * table_s[line + 2, k].astype(F32) + matrix(tile, rows_in)
            sums[k] = total.astype(BF16)
            return total
        lax.fori_loop(0, slots, step, jnp.zeros(sums.shape[1:], F32), unroll=8)

    products(0, dot, panel)

    def chunk(d, r):
        return turn(z, d, z_n) * 2 + (yh if r == 0 else 1 - yh)

    def sum_slot(d, r):
        return (1 - r) * z_n + SUM_ORDER.index(d)

    core_copy = {}
    for r in (1, 0):
        for first, end in ((0, 3), (3, z_n)):
            for d in SUM_ORDER[first:end]:
                part[sum_slot(d, r)] = sums[table_s[3, (1 - c) * (dest_n // 2) + chunk(d, r)]]
            span = pl.ds((1 - r) * z_n + first, end - first)
            core_copy[(r, first)] = put(part.at[span], core_in.at[span], core_peer)

    def own2(d, r):
        copy = core_copy.pop((r, 0 if d in SUM_ORDER[:3] else 3), None)
        if copy is not None:
            copy.wait_recv()
        return sums[table_s[3, c * (dest_n // 2) + chunk(d, r)]].astype(F32) + core_in[sum_slot(d, r)].astype(F32)

    def z_at(d):
        return at(z_=turn(z, d, z_n))

    mid = part.shape[1] // 2
    got = {}

    def far_dest(r):
        value = own2(4, r).astype(BF16)
        far_out[r] = value
        for i, way in enumerate((1, -1)):
            part_ref = pl.ds(i * mid, mid)
            got[(r, 4 * way)] = put(far_out.at[r, part_ref], far_in.at[r, part_ref], z_at(2 * way))
        for way in (1, -1):
            send(r, 3 * way, own2(3 * way, r), z_at(way))

    def send(r, d, value, device):
        i = r * 6 + {3: 0, -3: 1, 2: 2, -2: 3, 1: 4, -1: 5}[d]
        flow_out[i] = value.astype(BF16)
        got[(r, d)] = put(flow_out.at[i], flow_in.at[i], device)

    def came(r, d):
        got[(r, d)].wait_recv()
        return flow_in[r * 6 + {3: 0, -3: 1, 2: 2, -2: 3, 1: 4, -1: 5}[d]].astype(F32)

    def near_dest(r):
        for way in (1, -1):
            send(r, way, own2(way, r), z_at(way))

    def merged(r):
        for i, way in enumerate((1, -1)):
            value = own2(2 * way, r) + came(r, 3 * way)
            got[(r, 4 * way)].wait_recv()
            far = far_in[r, i * mid:(i + 1) * mid].astype(F32)
            if i == 0:
                value = jnp.concatenate([value[:mid] + far, value[mid:]], axis=0)
            else:
                value = jnp.concatenate([value[:mid], value[mid:] + far], axis=0)
            send(r, 2 * way, value, at(z_=turn(z, 2 * way, z_n), yh_=yh if r == 0 else 1 - yh))

    feats_on(1)
    far_dest(1)
    near_dest(1)
    far_dest(0)
    feats_on(2)
    merged(1)
    feats_on(3)
    yh_out[...] = (own2(0, 1) + came(1, 1) + came(1, -1)).astype(BF16)
    yh_copy = put(yh_out, yh_in, at(yh_=1 - yh))
    near_dest(0)
    merged(0)
    aggregate = own2(0, 0)
    for r, d in ((0, 1), (0, -1), (0, 2), (0, -2), (1, 2), (1, -2)):
        aggregate = aggregate + came(r, d)
    yh_copy.wait_recv()
    aggregate = aggregate + yh_in[...].astype(F32)

    deg = jnp.concatenate([deg_t[...]] * (aggregate.shape[1] // LANES), axis=1)
    preact = own_pre[...] + aggregate / deg
    sig = jax.nn.sigmoid(preact)
    dpre = cot_ref[...].astype(F32) * sig * (1.0 + preact * (1.0 - sig))
    dpre_b = dpre.astype(BF16)
    bands[c * (dest_n // 2)] = (dpre / deg).astype(BF16)

    def band(d, r):
        return bands.at[c * (dest_n // 2) + r * z_n + HAND_ORDER.index(d)]

    to_core = Bundle(bands.at[pl.ds(0, dest_n // 2)])
    hop = {}

    def core_too(r, first, end):
        ref = bands.at[pl.ds(c * (dest_n // 2) + r * z_n + first, end - first)]
        to_core.put(ref, ref, core_peer)

    def onward(r):
        for i, way in enumerate((1, -1)):
            hop[(r, 2 * way)].wait_recv()
            ref = band(-2 * way, r)
            rows_i = pl.ds(i * mid, mid)
            hop[(r, 4 * way)] = put(ref.at[rows_i], band(4, r).at[rows_i], z_at(2 * way))
            hop[(r, 3 * way)] = put(ref, band(-3 * way, r), z_at(way))

    def beside(r):
        for way in (1, -1):
            hop[(r, way)].wait_recv()
        core_too(r, 1, 5)

    def settle(r):
        for d in (3, -3, 4, -4):
            hop[(r, d)].wait_recv()
        core_too(r, 5, z_n)

    c_yh = put(band(0, 0), band(0, 1), at(yh_=1 - yh))
    for d in (2, -2, 1, -1):
        hop[(0, d)] = put(band(0, 0), band(-d, 0), z_at(d))
    core_too(0, 0, 1)
    node_ref[...] = (preact * sig).astype(BF16)
    save(node_ref, node_hbm)

    piece = feat_ref.shape[1] // (2 * X * z_n)
    f_half = feat_ref.shape[1] // 2
    f_x = f_half // X

    def all_reduce(i, value, side):
        if value is not None:
            fsum[i] = value
        e1_out[i] = fsum[i, pl.ds((1 - c) * f_half, f_half)].astype(BF16)
        copy = put(e1_out.at[i], e1_in.at[i], core_peer)
        if side is not None:
            o1[c] = side
            o_copy = put(o1.at[c], o1.at[c], core_peer)
        yield
        copy.wait_recv()
        fsum[i, 0:f_half] = fsum[i, pl.ds(c * f_half, f_half)] + e1_in[i].astype(F32)
        e2_out[i] = fsum[i, 0:f_half].astype(BF16)
        copies = Bundle(e2_in.at[i, pl.ds(1, X - 1)])
        for d in far_first(X):
            there = turn(x, d, X)
            copies.put(e2_out.at[i, pl.ds(there * f_x, f_x)], e2_in.at[i, d], at(x_=there))
        if side is not None:
            o_copy.wait_recv()
            o2[x] = jnp.sum(o1[...], axis=0)
            o_copy = put_all(o2.at[pl.ds(0, X - 1)], o2.at[x], x_peers)
        yield
        total = fsum[i, pl.ds(x * f_x, f_x)]
        copies.wait_recv()
        for d in range(1, X):
            total = total + e2_in[i, d].astype(F32)
        fsum[i, 0:f_x] = total
        e3_out[i] = total.astype(BF16)
        copies = Bundle(e3_in.at[i, pl.ds(1, z_n - 1)])
        for d in far_first(z_n):
            there = turn(z, d, z_n)
            copies.put(e3_out.at[i, pl.ds(there * piece, piece)], e3_in.at[i, d], at(z_=there))
        if side is not None:
            o_copy.wait_recv()
            o3[z] = jnp.sum(o2[...], axis=0)
            o_copy = put_all(o3.at[pl.ds(0, z_n - 1)], o3.at[z], z_peers)
        yield
        total = fsum[i, pl.ds(z * piece, piece)]
        copies.wait_recv()
        for d in range(1, z_n):
            total = total + e3_in[i, d].astype(F32)
        e4[i, y] = total.astype(BF16)
        copies = put_all(e4.at[i, pl.ds(0, y_n - 1)], e4.at[i, y], y_peers)
        if side is not None:
            o_copy.wait_recv()
            o4[y] = jnp.sum(o3[...], axis=0)
            o_copy = put_all(o4.at[pl.ds(0, y_n - 1)], o4.at[y], y_peers)
        yield
        copies.wait_recv()
        total = e4[i, 0].astype(F32)
        for there in range(1, y_n):
            total = total + e4[i, there].astype(F32)
        start = c * f_half + x * f_x + z * piece
        egather[i, pl.ds(start, piece)] = (total * scale).astype(BF16)
        ref = egather.at[i, pl.ds(start, piece)]
        copies = put_all(egather.at[i, pl.ds(0, (z_n - 1) * piece)], ref, z_peers)
        if side is not None:
            o_copy.wait_recv()
            ograd_ref[...] = (jnp.sum(o4[...], axis=0) * scale)[0:1]
            save(ograd_ref, ograd_hbm)
        yield
        copies.wait_recv()
        ref = egather.at[i, pl.ds(c * f_half + x * f_x, f_x)]
        copies = put_all(egather.at[i, pl.ds(0, (X - 1) * f_x)], ref, x_peers)
        yield
        copies.wait_recv()
        ref = egather.at[i, pl.ds(c * f_half, f_half)]
        copy = put(ref, ref, core_peer)
        yield
        copy.wait_recv()
        save(egather.at[i], sgrad_hbm if i == 0 else ngrad_hbm)

    side = jnp.broadcast_to(jnp.sum(dpre, axis=0, keepdims=True), o1.shape[1:])
    self_steps = all_reduce(0, dot(feats_t[x * yl_n + yl], dpre_b), side)
    next(self_steps)

    own_pre[...] = dpre
    c_yh.wait_recv()
    for d in (2, -2):
        hop[(1, d)] = put(band(0, 1), band(-d, 1), z_at(d))
    onward(0)
    for d in (1, -1):
        hop[(1, d)] = put(band(0, 1), band(-d, 1), z_at(d))
    core_too(1, 0, 1)
    beside(0)
    onward(1)
    settle(0)
    next(self_steps)
    beside(1)
    settle(1)
    to_core.wait_recv()

    products(4, dot_t, bands)

    def take_back(q, _):
        back[q] = sums[table_s[7, q]]
        return 0
    lax.fori_loop(0, src_n, take_back, 0)

    def back_at(dx, d):
        return turn(x, dx, X) * yl_n + mate(d)

    f_ring.wait_recv()

    def share(m, _):
        at_m = pl.ds(pl.multiple_of(m * LANES, LANES), LANES)
        total = jnp.zeros((LANES, back.shape[2]), F32)
        for q in range(0, src_n, 2):
            left_in = jnp.concatenate([feats_t[q, at_m], feats_t[q + 1, at_m]], axis=1)
            right_in = back[q:q + 2].reshape(2 * back.shape[1], back.shape[2])
            total = total + dot(left_in, right_in)
        fsum[1, at_m] = total
        return 0
    f_tiles = f_half // LANES
    lax.fori_loop((1 - c) * f_tiles, (2 - c) * f_tiles, share, 0)
    neigh_steps = all_reduce(1, None, None)
    next(neigh_steps)
    lax.fori_loop(c * f_tiles, (1 + c) * f_tiles, share, 0)
    drain(12)
    next(self_steps)
    next(neigh_steps)

    order = [3, 2, 1, 0]
    ring = {}
    for d in order:
        for dx in far_first(X):
            ring[(dx, d)] = put(back.at[back_at(dx, d)], ring_in.at[dx - 1, d], at(x_=turn(x, dx, X)))
    next(self_steps)
    next(neigh_steps)
    drain(24)
    next(self_steps)
    next(neigh_steps)
    y_copy = {}
    for d in order:
        value = back[back_at(0, d)].astype(F32)
        for dx in range(1, X):
            ring[(dx, d)].wait_recv()
            value = value + ring_in[dx - 1, d].astype(F32)
        if d > 0:
            line_out[d] = value.astype(BF16)
            y_copy[d] = put(line_out.at[d], line_in.at[d], at(yl_=mate(d)))
        else:
            dprop = value
    next(self_steps)
    next(neigh_steps)
    drain(8)
    for d in range(1, yl_n):
        y_copy[d].wait_recv()
        dprop = dprop + line_in[d].astype(F32)
    fgrad_ref[...] = (
        dot_nt(own_pre[...].astype(BF16), ws_ref[...]) + dot_nt(dprop.astype(BF16), wn_ref[...])
    ).astype(BF16)
    save(fgrad_ref, fgrad_hbm)
    next(self_steps)
    next(neigh_steps)
    next(self_steps, None)
    drain(3)
    next(neigh_steps)
    drain(1)
    next(neigh_steps, None)
    drain(0)
    for copy in saved:
        copy.wait()


def hand_on(*refs):
    count = (len(refs) - 2) // 3
    there, here, held = refs[:count], refs[count:2 * count], refs[2 * count:3 * count]
    sem_in, sem_out = refs[-2:]
    fetch = [pltpu.make_async_copy(there[i], held[i], sem_in.at[i]) for i in range(count)]
    store = [pltpu.make_async_copy(held[i], here[i], sem_out.at[i]) for i in range(count)]
    for copy in fetch:
        copy.start()
    for i in range(count):
        fetch[i].wait()
        store[i].start()
    for copy in store:
        copy.wait()


def run(rows, cols, features, degree, blocks, coords, counts, w_self, w_neigh, offset, cotangent):
    nodes_dev, hidden = cotangent.shape
    width = features.shape[1]
    slots, side = blocks.shape[2], blocks.shape[3]
    z_n, yl_n = cols // 4, rows // X
    y_n = 2 * yl_n
    f_half = width // 2
    f_x = f_half // X
    piece = f_x // z_n
    scale = 1.0 / math.sqrt(nodes_dev * rows * cols)
    hbm = pl.BlockSpec(memory_space=pl.ANY)
    block = (side, hidden)
    copies = 80
    scratch = [
        pltpu.VMEM((nodes_dev, hidden), BF16),
        pltpu.VMEM((nodes_dev, width), BF16),
        pltpu.VMEM((1, hidden), F32),
        pltpu.VMEM((rows, width, nodes_dev), BF16),
        pltpu.VMEM((LANES, LANES), F32),
        pltpu.VMEM((nodes_dev, width), BF16),
        pltpu.VMEM((1, nodes_dev), jnp.int32),
        pltpu.VMEM((slots, side, side), BF16),
        pltpu.VMEM((1, slots), jnp.int32),
        pltpu.SMEM((1, 1), jnp.int32),
        pltpu.VMEM((width, hidden), BF16),
        pltpu.VMEM((width, hidden), BF16),
        pltpu.VMEM((hidden // LANES, LANES), BF16),
        pltpu.VMEM((nodes_dev, hidden), BF16),
        pltpu.VMEM((rows,) + block, BF16),
        pltpu.VMEM((slots + 1,) + block, BF16),
        pltpu.VMEM((cols // 2,) + block, BF16),
        pltpu.VMEM((cols // 2,) + block, BF16),
        pltpu.VMEM((12,) + block, BF16),
        pltpu.VMEM((12,) + block, BF16),
        pltpu.VMEM((2,) + block, BF16),
        pltpu.VMEM((2,) + block, BF16),
        pltpu.VMEM(block, BF16),
        pltpu.VMEM(block, BF16),
        pltpu.VMEM((cols,) + block, BF16),
        pltpu.VMEM((rows,) + block, BF16),
        pltpu.VMEM((3, yl_n) + block, BF16),
        pltpu.VMEM((yl_n,) + block, BF16),
        pltpu.VMEM((yl_n,) + block, BF16),
        pltpu.VMEM((nodes_dev, hidden), F32),
        pltpu.VMEM((2, width, hidden), F32),
        pltpu.VMEM((2, f_half, hidden), BF16),
        pltpu.VMEM((2, f_half, hidden), BF16),
        pltpu.VMEM((2, f_half, hidden), BF16),
        pltpu.VMEM((2, X, f_x, hidden), BF16),
        pltpu.VMEM((2, f_x, hidden), BF16),
        pltpu.VMEM((2, z_n, piece, hidden), BF16),
        pltpu.VMEM((2, y_n, piece, hidden), BF16),
        pltpu.VMEM((2, width, hidden), BF16),
        pltpu.VMEM((2, 8, hidden), F32),
        pltpu.VMEM((X, 8, hidden), F32),
        pltpu.VMEM((z_n, 8, hidden), F32),
        pltpu.VMEM((y_n, 8, hidden), F32),
        pltpu.VMEM((8, LANES), jnp.int32),
        pltpu.SMEM((8, LANES), jnp.int32),
        pltpu.SemaphoreType.DMA((10,)),
        pltpu.SemaphoreType.DMA((5,)),
        pltpu.SemaphoreType.DMA((SEND_POOL,)),
        pltpu.SemaphoreType.DMA((copies,)),
    ]
    shapes = (
            jax.ShapeDtypeStruct((nodes_dev, hidden), BF16),
            jax.ShapeDtypeStruct((nodes_dev, width), BF16),
            jax.ShapeDtypeStruct((width, hidden), BF16),
            jax.ShapeDtypeStruct((width, hidden), BF16),
            jax.ShapeDtypeStruct((1, hidden), F32),
        )
    results = pl.pallas_call(
        functools.partial(kernel, rows, cols, slots, scale),
        out_shape=shapes,
        in_specs=[hbm] * 9,
        out_specs=[hbm] * 5,
        scratch_shapes=scratch,
        compiler_params=pltpu.CompilerParams(
            collective_id=0, has_side_effects=True, vmem_limit_bytes=60 * 1024 * 1024
        ),
    )(
        features, degree.reshape(1, nodes_dev), blocks.reshape(slots, side, side),
        coords.reshape(1, slots), counts, w_self, w_neigh, offset.reshape(hidden // LANES, LANES), cotangent,
    )
    node_out, feat_grad, self_grad, neigh_grad, offset_grad = pl.pallas_call(
        hand_on,
        out_shape=shapes,
        in_specs=[hbm] * 5,
        out_specs=[hbm] * 5,
        scratch_shapes=[pltpu.VMEM(held.shape, held.dtype) for held in shapes]
        + [pltpu.SemaphoreType.DMA((5,)), pltpu.SemaphoreType.DMA((5,))],
        compiler_params=pltpu.CompilerParams(vmem_limit_bytes=60 * 1024 * 1024),
    )(*results)
    return node_out, feat_grad, self_grad, neigh_grad, offset_grad.reshape(hidden)


def solution(mesh):
    return jax.shard_map(
        functools.partial(run, mesh.shape["row"], mesh.shape["col"]),
        mesh=mesh,
        in_specs=(
            P(("row", "col"), None),
            P(("row", "col")),
            P("row", "col", None, None, None),
            P("row", "col", None),
            P("row", "col"),
            P(),
            P(),
            P(),
            P(("row", "col"), None),
        ),
        out_specs=(P(("row", "col"), None), P(("row", "col"), None), P(), P(), P()),
        check_vma=False,
    )
```

```python
import functools
import math

import jax
import jax.numpy as jnp
from jax import lax
from jax.experimental import pallas as pl
from jax.experimental.pallas import tpu as pltpu
from jax.sharding import PartitionSpec as P

MESH = pl.DeviceIdType.MESH
BF16 = jnp.bfloat16
F32 = jnp.float32
X = 4
LANES = 128
SUM_ORDER = (4, 3, -3, 1, -1, 2, -2, 0)
HAND_ORDER = (0, 2, -2, 1, -1, 3, -3, 4)
BIG = 1 << 20
SEND_POOL = 48


def spread_t(row):
    return jnp.broadcast_to(row, (LANES, LANES)).T


def slot_tables(group, other, used, slots):
    lane = lax.broadcasted_iota(jnp.int32, (LANES, LANES), 1)
    sub = lax.broadcasted_iota(jnp.int32, (LANES, LANES), 0)
    key = jnp.where(used > 0, group * LANES + lane[:1], BIG + lane[:1])
    key_r = jnp.broadcast_to(key, (LANES, LANES))
    key_c = spread_t(key)
    grp_r = jnp.broadcast_to(group, (LANES, LANES))
    grp_c = spread_t(group)
    used_c = spread_t(used)
    other_c = spread_t(other)
    less = jnp.where(key_r < key_c, 1, 0)
    rank = jnp.sum(less, axis=1, keepdims=True)
    same = jnp.where(grp_r == grp_c, less, 0)
    keep = jnp.minimum(jnp.sum(same, axis=1, keepdims=True), 1)
    hot = rank == lane
    order = jnp.sum(jnp.where(hot, sub, 0), axis=0, keepdims=True)
    there = jnp.sum(jnp.where(hot, other_c, 0), axis=0, keepdims=True)
    keeps = jnp.sum(jnp.where(hot, keep, 0), axis=0, keepdims=True)
    upto = jnp.sum(jnp.where(grp_c <= lane, used_c, 0), axis=0, keepdims=True)
    here = jnp.sum(jnp.where(grp_c == lane, used_c, 0), axis=0, keepdims=True)
    last = jnp.where(here > 0, upto - 1, slots)
    return [order, there, keeps, last]


def kernel(
    rows, cols, slots, scale,
    feat_hbm, deg_hbm, blocks_hbm, coords_hbm, counts_hbm, ws_hbm, wn_hbm, off_hbm, cot_hbm,
    node_hbm, fgrad_hbm, sgrad_hbm, ngrad_hbm, ograd_hbm,
    node_ref, fgrad_ref, ograd_ref, feats_t, deg_t,
    feat_ref, deg_ref, tiles, coords_ref, counts_ref, ws_ref, wn_ref, off_ref, cot_ref,
    panel, sums, part, core_in, flow_out, flow_in, far_out, far_in, yh_out, yh_in, bands, back,
    ring_in, line_out, line_in, own_pre, fsum,
    e1_out, e1_in, e2_out, e2_in, e3_out, e3_in, e4, egather, o1, o2, o3, o4,
    table_v, table_s, copy_sem, out_sem, send_sem, recv_sem,
):
    yl_n = rows // X
    z_n = cols // 4
    row = lax.axis_index("row")
    col = lax.axis_index("col")
    x = lax.rem(row, X)
    yl = row // X
    z = col // 4
    yh = lax.rem(col // 2, 2)
    c = lax.rem(col, 2)
    src_n = rows
    dest_n = cols

    def at(yl_=None, x_=None, z_=None, yh_=None, c_=None):
        yl_ = yl if yl_ is None else yl_
        x_ = x if x_ is None else x_
        z_ = z if z_ is None else z_
        yh_ = yh if yh_ is None else yh_
        c_ = c if c_ is None else c_
        return (yl_ * X + x_, z_ * 4 + yh_ * 2 + c_)

    def turn(i, d, n):
        return lax.rem(i + (d % n), n)

    y_n = 2 * yl_n
    y = yh * yl_n + yl

    def at_y(y_):
        return at(yl_=lax.rem(y_, yl_n), yh_=y_ // yl_n)

    def far_first(n):
        return sorted(range(1, n), key=lambda d: -min(d, n - d))

    x_peers = [at(x_=turn(x, d, X)) for d in far_first(X)]
    z_peers = [at(z_=turn(z, d, z_n)) for d in far_first(z_n)]
    y_peers = [at_y(turn(y, d, y_n)) for d in far_first(y_n)]
    core_peer = at(c_=1 - c)
    peers = z_peers + y_peers + x_peers + [core_peer]

    away = range(1, yl_n)

    def mate(d):
        if d == 1:
            return yl + 1 - 2 * lax.rem(yl, 2)
        if d == 2:
            return lax.rem(yl + 2, 4)
        return 3 - yl if d == 3 else yl

    issued = []
    drained = [0]

    def drain(keep):
        while drained[0] < len(issued) - keep:
            issued[drained[0]].wait_send()
            drained[0] += 1

    def next_slot(message):
        issued.append(message)
        drain(SEND_POOL)
        i = len(issued) - 1
        return send_sem.at[i % SEND_POOL], recv_sem.at[i]

    class Bundle:
        def __init__(self, span):
            self.span = span
            self.send, self.recv = next_slot(self)

        def put(self, src, dst, device):
            pltpu.make_async_remote_copy(
                src_ref=src, dst_ref=dst, send_sem=self.send, recv_sem=self.recv,
                device_id=device, device_id_type=MESH,
            ).start()

        def wait_recv(self):
            pltpu.make_async_copy(self.span, self.span, self.recv).wait()

        def wait_send(self):
            pltpu.make_async_copy(self.span, self.span, self.send).wait()

    def put(src, dst, device):
        message = Bundle(dst)
        message.put(src, dst, device)
        return message

    def put_all(span, ref, devices):
        bundle = Bundle(span)
        for device in devices:
            bundle.put(ref, ref, device)
        return bundle

    saved = []

    def save(src, dst):
        copy = pltpu.make_async_copy(src, dst, out_sem.at[len(saved)])
        copy.start()
        saved.append(copy)

    def dot(a, b):
        return jnp.dot(a, b, preferred_element_type=F32)

    def dot_t(a, b):
        return lax.dot_general(a, b, (((0,), (0,)), ((), ())), preferred_element_type=F32)

    def dot_nt(a, b):
        return lax.dot_general(a, b, (((1,), (1,)), ((), ())), preferred_element_type=F32)

    barrier = pltpu.get_barrier_semaphore()
    for peer in peers:
        pl.semaphore_signal(barrier, inc=1, device_id=peer, device_id_type=MESH)
    loads = {}
    for i, (name, there, here) in enumerate((
        ("feat", feat_hbm, feat_ref), ("wn", wn_hbm, wn_ref), ("coords", coords_hbm, coords_ref),
        ("counts", counts_hbm, counts_ref), ("ws", ws_hbm, ws_ref), ("off", off_hbm, off_ref),
        ("tiles", blocks_hbm, tiles), ("deg", deg_hbm, deg_ref), ("cot", cot_hbm, cot_ref),
    )):
        loads[name] = pltpu.make_async_copy(there, here, copy_sem.at[i])
        loads[name].start()
    loads["feat"].wait()
    loads["wn"].wait()
    panel[x * yl_n + yl] = dot(feat_ref[...], wn_ref[...]).astype(BF16)
    pl.semaphore_wait(barrier, len(peers))

    mine = panel.at[x * yl_n + yl]
    a_line = {d: put(mine, mine, at(yl_=mate(d))) for d in away}
    a_ring = put_all(panel.at[pl.ds(0, (X - 1) * yl_n)], mine, x_peers)

    loads["coords"].wait()
    loads["counts"].wait()
    table_v[...] = jnp.zeros_like(table_v)
    table_v[0:1, 0:slots] = coords_ref[...]
    code = table_v[0:1, :]
    lane = lax.broadcasted_iota(jnp.int32, (1, LANES), 1)
    used = jnp.where(lane < counts_ref[0, 0], 1, 0)
    src_bits = (src_n - 1).bit_length()
    dest = lax.shift_right_logical(code, src_bits)
    src = lax.bitwise_and(code, src_n - 1)
    dest_q = lax.bitwise_and(dest, 1) * (dest_n // 2) + lax.shift_right_logical(dest, 1)
    src_q = lax.bitwise_and(src, X - 1) * yl_n + lax.shift_right_logical(src, 2)
    lines = slot_tables(dest_q, src_q, used, slots)
    away_z = lax.rem(lax.shift_right_logical(dest, 2) - z + z_n, z_n)
    place = jnp.zeros_like(away_z)
    for i, d in enumerate(HAND_ORDER):
        place = jnp.where(away_z == d % z_n, i, place)
    other_yh = jnp.where(lax.bitwise_and(lax.shift_right_logical(dest, 1), 1) == yh, 0, z_n)
    hand_q = lax.bitwise_and(dest, 1) * (dest_n // 2) + other_yh + place
    lines += slot_tables(src_q, hand_q, used, slots)
    for i, line in enumerate(lines):
        table_v[i:i + 1, :] = line
    table_copy = pltpu.make_async_copy(table_v, table_s, copy_sem.at[9])
    table_copy.start()

    for d in away:
        a_line[d].wait_recv()
        ref = panel.at[x * yl_n + mate(d)]
        for peer in x_peers:
            a_ring.put(ref, ref, peer)
    feats_t[x * yl_n + yl] = feat_ref[...].T
    mine_t = feats_t.at[x * yl_n + yl]
    f_line = {d: put(mine_t, mine_t, at(yl_=mate(d))) for d in away}
    loads["ws"].wait()
    loads["off"].wait()
    off = jnp.concatenate([off_ref[i:i + 1, :] for i in range(off_ref.shape[0])], axis=1)
    own_pre[...] = dot(feat_ref[...], ws_ref[...]) + off.astype(F32)
    sums[slots] = jnp.zeros_like(sums[slots])
    loads["tiles"].wait()
    loads["deg"].wait()
    loads["cot"].wait()
    deg_t[...] = spread_t(deg_ref[...].astype(F32))
    table_copy.wait()
    a_ring.wait_recv()

    f_ring = put_all(feats_t.at[pl.ds(0, (X - 1) * yl_n)], mine_t, x_peers)

    def feats_on(d):
        f_line[d].wait_recv()
        ref = feats_t.at[x * yl_n + mate(d)]
        for peer in x_peers:
            f_ring.put(ref, ref, peer)

    def products(line, matrix, operand):
        def step(k, total):
            tile = tiles[table_s[line, k]]
            rows_in = operand[table_s[line + 1, k]]
            total = total * table_s[line + 2, k].astype(F32) + matrix(tile, rows_in)
            sums[k] = total.astype(BF16)
            return total
        lax.fori_loop(0, slots, step, jnp.zeros(sums.shape[1:], F32), unroll=8)

    products(0, dot, panel)

    def chunk(d, r):
        return turn(z, d, z_n) * 2 + (yh if r == 0 else 1 - yh)

    def sum_slot(d, r):
        return (1 - r) * z_n + SUM_ORDER.index(d)

    core_copy = {}
    for r in (1, 0):
        for first, end in ((0, 3), (3, z_n)):
            for d in SUM_ORDER[first:end]:
                part[sum_slot(d, r)] = sums[table_s[3, (1 - c) * (dest_n // 2) + chunk(d, r)]]
            span = pl.ds((1 - r) * z_n + first, end - first)
            core_copy[(r, first)] = put(part.at[span], core_in.at[span], core_peer)

    def own2(d, r):
        copy = core_copy.pop((r, 0 if d in SUM_ORDER[:3] else 3), None)
        if copy is not None:
            copy.wait_recv()
        return sums[table_s[3, c * (dest_n // 2) + chunk(d, r)]].astype(F32) + core_in[sum_slot(d, r)].astype(F32)

    def z_at(d):
        return at(z_=turn(z, d, z_n))

    mid = part.shape[1] // 2
    got = {}

    def far_dest(r):
        value = own2(4, r).astype(BF16)
        far_out[r] = value
        for i, way in enumerate((1, -1)):
            part_ref = pl.ds(i * mid, mid)
            got[(r, 4 * way)] = put(far_out.at[r, part_ref], far_in.at[r, part_ref], z_at(2 * way))
        for way in (1, -1):
            send(r, 3 * way, own2(3 * way, r), z_at(way))

    def send(r, d, value, device):
        i = r * 6 + {3: 0, -3: 1, 2: 2, -2: 3, 1: 4, -1: 5}[d]
        flow_out[i] = value.astype(BF16)
        got[(r, d)] = put(flow_out.at[i], flow_in.at[i], device)

    def came(r, d):
        got[(r, d)].wait_recv()
        return flow_in[r * 6 + {3: 0, -3: 1, 2: 2, -2: 3, 1: 4, -1: 5}[d]].astype(F32)

    def near_dest(r):
        for way in (1, -1):
            send(r, way, own2(way, r), z_at(way))

    def merged(r):
        for i, way in enumerate((1, -1)):
            value = own2(2 * way, r) + came(r, 3 * way)
            got[(r, 4 * way)].wait_recv()
            far = far_in[r, i * mid:(i + 1) * mid].astype(F32)
            if i == 0:
                value = jnp.concatenate([value[:mid] + far, value[mid:]], axis=0)
            else:
                value = jnp.concatenate([value[:mid], value[mid:] + far], axis=0)
            send(r, 2 * way, value, z_at(2 * way))

    feats_on(1)
    far_dest(1)
    near_dest(1)
    far_dest(0)
    feats_on(2)
    merged(1)
    feats_on(3)
    near_dest(0)
    merged(0)
    others = own2(0, 1)
    for d in (1, -1, 2, -2):
        others = others + came(1, d)
    yh_out[...] = others.astype(BF16)
    yh_copy = put(yh_out, yh_in, at(yh_=1 - yh))
    aggregate = own2(0, 0)
    for d in (1, -1, 2, -2):
        aggregate = aggregate + came(0, d)
    yh_copy.wait_recv()
    aggregate = aggregate + yh_in[...].astype(F32)

    deg = jnp.concatenate([deg_t[...]] * (aggregate.shape[1] // LANES), axis=1)
    preact = own_pre[...] + aggregate / deg
    sig = jax.nn.sigmoid(preact)
    dpre = cot_ref[...].astype(F32) * sig * (1.0 + preact * (1.0 - sig))
    dpre_b = dpre.astype(BF16)
    bands[c * (dest_n // 2)] = (dpre / deg).astype(BF16)

    def band(d, r):
        return bands.at[c * (dest_n // 2) + r * z_n + HAND_ORDER.index(d)]

    to_core = Bundle(bands.at[pl.ds(0, dest_n // 2)])
    hop = {}

    def core_too(r, first, end):
        ref = bands.at[pl.ds(c * (dest_n // 2) + r * z_n + first, end - first)]
        to_core.put(ref, ref, core_peer)

    def onward(r):
        for i, way in enumerate((1, -1)):
            hop[(r, 2 * way)].wait_recv()
            ref = band(-2 * way, r)
            rows_i = pl.ds(i * mid, mid)
            hop[(r, 4 * way)] = put(ref.at[rows_i], band(4, r).at[rows_i], z_at(2 * way))
            hop[(r, 3 * way)] = put(ref, band(-3 * way, r), z_at(way))

    def beside(r):
        for way in (1, -1):
            hop[(r, way)].wait_recv()
        core_too(r, 1, 5)

    def settle(r):
        for d in (3, -3, 4, -4):
            hop[(r, d)].wait_recv()
        core_too(r, 5, z_n)

    c_yh = put(band(0, 0), band(0, 1), at(yh_=1 - yh))
    for d in (2, -2, 1, -1):
        hop[(0, d)] = put(band(0, 0), band(-d, 0), z_at(d))
    core_too(0, 0, 1)
    node_ref[...] = (preact * sig).astype(BF16)
    save(node_ref, node_hbm)

    piece = feat_ref.shape[1] // (2 * X * z_n)
    f_half = feat_ref.shape[1] // 2
    f_x = f_half // X

    def all_reduce(i, value, side):
        if value is not None:
            fsum[i] = value
        e1_out[i] = fsum[i, pl.ds((1 - c) * f_half, f_half)].astype(BF16)
        copy = put(e1_out.at[i], e1_in.at[i], core_peer)
        if side is not None:
            o1[c] = side
            o_copy = put(o1.at[c], o1.at[c], core_peer)
        yield
        copy.wait_recv()
        fsum[i, 0:f_half] = fsum[i, pl.ds(c * f_half, f_half)] + e1_in[i].astype(F32)
        e2_out[i] = fsum[i, 0:f_half].astype(BF16)
        copies = Bundle(e2_in.at[i, pl.ds(1, X - 1)])
        for d in far_first(X):
            there = turn(x, d, X)
            copies.put(e2_out.at[i, pl.ds(there * f_x, f_x)], e2_in.at[i, d], at(x_=there))
        if side is not None:
            o_copy.wait_recv()
            o2[x] = jnp.sum(o1[...], axis=0)
            o_copy = put_all(o2.at[pl.ds(0, X - 1)], o2.at[x], x_peers)
        yield
        total = fsum[i, pl.ds(x * f_x, f_x)]
        copies.wait_recv()
        for d in range(1, X):
            total = total + e2_in[i, d].astype(F32)
        fsum[i, 0:f_x] = total
        e3_out[i] = total.astype(BF16)
        copies = Bundle(e3_in.at[i, pl.ds(1, z_n - 1)])
        for d in far_first(z_n):
            there = turn(z, d, z_n)
            copies.put(e3_out.at[i, pl.ds(there * piece, piece)], e3_in.at[i, d], at(z_=there))
        if side is not None:
            o_copy.wait_recv()
            o3[z] = jnp.sum(o2[...], axis=0)
            o_copy = put_all(o3.at[pl.ds(0, z_n - 1)], o3.at[z], z_peers)
        yield
        total = fsum[i, pl.ds(z * piece, piece)]
        copies.wait_recv()
        for d in range(1, z_n):
            total = total + e3_in[i, d].astype(F32)
        e4[i, y] = total.astype(BF16)
        copies = put_all(e4.at[i, pl.ds(0, y_n - 1)], e4.at[i, y], y_peers)
        if side is not None:
            o_copy.wait_recv()
            o4[y] = jnp.sum(o3[...], axis=0)
            o_copy = put_all(o4.at[pl.ds(0, y_n - 1)], o4.at[y], y_peers)
        yield
        copies.wait_recv()
        total = e4[i, 0].astype(F32)
        for there in range(1, y_n):
            total = total + e4[i, there].astype(F32)
        start = c * f_half + x * f_x + z * piece
        egather[i, pl.ds(start, piece)] = (total * scale).astype(BF16)
        ref = egather.at[i, pl.ds(start, piece)]
        copies = put_all(egather.at[i, pl.ds(0, (z_n - 1) * piece)], ref, z_peers)
        if side is not None:
            o_copy.wait_recv()
            ograd_ref[...] = (jnp.sum(o4[...], axis=0) * scale)[0:1]
            save(ograd_ref, ograd_hbm)
        yield
        copies.wait_recv()
        ref = egather.at[i, pl.ds(c * f_half + x * f_x, f_x)]
        copies = put_all(egather.at[i, pl.ds(0, (X - 1) * f_x)], ref, x_peers)
        yield
        copies.wait_recv()
        ref = egather.at[i, pl.ds(c * f_half, f_half)]
        copy = put(ref, ref, core_peer)
        yield
        copy.wait_recv()
        save(egather.at[i], sgrad_hbm if i == 0 else ngrad_hbm)

    side = jnp.broadcast_to(jnp.sum(dpre, axis=0, keepdims=True), o1.shape[1:])
    self_steps = all_reduce(0, dot(feats_t[x * yl_n + yl], dpre_b), side)
    next(self_steps)

    own_pre[...] = dpre
    c_yh.wait_recv()
    for d in (2, -2):
        hop[(1, d)] = put(band(0, 1), band(-d, 1), z_at(d))
    onward(0)
    for d in (1, -1):
        hop[(1, d)] = put(band(0, 1), band(-d, 1), z_at(d))
    core_too(1, 0, 1)
    beside(0)
    onward(1)
    settle(0)
    next(self_steps)
    beside(1)
    settle(1)
    to_core.wait_recv()

    products(4, dot_t, bands)

    def take_back(q, _):
        back[q] = sums[table_s[7, q]]
        return 0
    lax.fori_loop(0, src_n, take_back, 0)

    def back_at(dx, d):
        return turn(x, dx, X) * yl_n + mate(d)

    f_ring.wait_recv()

    def share(m, _):
        at_m = pl.ds(pl.multiple_of(m * LANES, LANES), LANES)
        total = jnp.zeros((LANES, back.shape[2]), F32)
        for q in range(0, src_n, 2):
            left_in = jnp.concatenate([feats_t[q, at_m], feats_t[q + 1, at_m]], axis=1)
            right_in = back[q:q + 2].reshape(2 * back.shape[1], back.shape[2])
            total = total + dot(left_in, right_in)
        fsum[1, at_m] = total
        return 0
    f_tiles = f_half // LANES
    lax.fori_loop((1 - c) * f_tiles, (2 - c) * f_tiles, share, 0)
    neigh_steps = all_reduce(1, None, None)
    next(neigh_steps)
    lax.fori_loop(c * f_tiles, (1 + c) * f_tiles, share, 0)
    drain(12)
    next(self_steps)
    next(neigh_steps)

    order = [3, 2, 1, 0]
    ring = {}
    for d in order:
        for dx in far_first(X):
            ring[(dx, d)] = put(back.at[back_at(dx, d)], ring_in.at[dx - 1, d], at(x_=turn(x, dx, X)))
    next(self_steps)
    next(neigh_steps)
    drain(24)
    next(self_steps)
    next(neigh_steps)
    y_copy = {}
    for d in order:
        value = back[back_at(0, d)].astype(F32)
        for dx in range(1, X):
            ring[(dx, d)].wait_recv()
            value = value + ring_in[dx - 1, d].astype(F32)
        if d > 0:
            line_out[d] = value.astype(BF16)
            y_copy[d] = put(line_out.at[d], line_in.at[d], at(yl_=mate(d)))
        else:
            dprop = value
    next(self_steps)
    next(neigh_steps)
    drain(8)
    for d in range(1, yl_n):
        y_copy[d].wait_recv()
        dprop = dprop + line_in[d].astype(F32)
    fgrad_ref[...] = (
        dot_nt(own_pre[...].astype(BF16), ws_ref[...]) + dot_nt(dprop.astype(BF16), wn_ref[...])
    ).astype(BF16)
    save(fgrad_ref, fgrad_hbm)
    next(self_steps)
    next(neigh_steps)
    next(self_steps, None)
    drain(3)
    next(neigh_steps)
    drain(1)
    next(neigh_steps, None)
    drain(0)
    for copy in saved:
        copy.wait()


def hand_on(*refs):
    count = (len(refs) - 2) // 3
    there, here, held = refs[:count], refs[count:2 * count], refs[2 * count:3 * count]
    sem_in, sem_out = refs[-2:]
    fetch = [pltpu.make_async_copy(there[i], held[i], sem_in.at[i]) for i in range(count)]
    store = [pltpu.make_async_copy(held[i], here[i], sem_out.at[i]) for i in range(count)]
    for copy in fetch:
        copy.start()
    for i in range(count):
        fetch[i].wait()
        store[i].start()
    for copy in store:
        copy.wait()


def run(rows, cols, features, degree, blocks, coords, counts, w_self, w_neigh, offset, cotangent):
    nodes_dev, hidden = cotangent.shape
    width = features.shape[1]
    slots, side = blocks.shape[2], blocks.shape[3]
    z_n, yl_n = cols // 4, rows // X
    y_n = 2 * yl_n
    f_half = width // 2
    f_x = f_half // X
    piece = f_x // z_n
    scale = 1.0 / math.sqrt(nodes_dev * rows * cols)
    hbm = pl.BlockSpec(memory_space=pl.ANY)
    block = (side, hidden)
    copies = 80
    scratch = [
        pltpu.VMEM((nodes_dev, hidden), BF16),
        pltpu.VMEM((nodes_dev, width), BF16),
        pltpu.VMEM((1, hidden), F32),
        pltpu.VMEM((rows, width, nodes_dev), BF16),
        pltpu.VMEM((LANES, LANES), F32),
        pltpu.VMEM((nodes_dev, width), BF16),
        pltpu.VMEM((1, nodes_dev), jnp.int32),
        pltpu.VMEM((slots, side, side), BF16),
        pltpu.VMEM((1, slots), jnp.int32),
        pltpu.SMEM((1, 1), jnp.int32),
        pltpu.VMEM((width, hidden), BF16),
        pltpu.VMEM((width, hidden), BF16),
        pltpu.VMEM((hidden // LANES, LANES), BF16),
        pltpu.VMEM((nodes_dev, hidden), BF16),
        pltpu.VMEM((rows,) + block, BF16),
        pltpu.VMEM((slots + 1,) + block, BF16),
        pltpu.VMEM((cols // 2,) + block, BF16),
        pltpu.VMEM((cols // 2,) + block, BF16),
        pltpu.VMEM((12,) + block, BF16),
        pltpu.VMEM((12,) + block, BF16),
        pltpu.VMEM((2,) + block, BF16),
        pltpu.VMEM((2,) + block, BF16),
        pltpu.VMEM(block, BF16),
        pltpu.VMEM(block, BF16),
        pltpu.VMEM((cols,) + block, BF16),
        pltpu.VMEM((rows,) + block, BF16),
        pltpu.VMEM((3, yl_n) + block, BF16),
        pltpu.VMEM((yl_n,) + block, BF16),
        pltpu.VMEM((yl_n,) + block, BF16),
        pltpu.VMEM((nodes_dev, hidden), F32),
        pltpu.VMEM((2, width, hidden), F32),
        pltpu.VMEM((2, f_half, hidden), BF16),
        pltpu.VMEM((2, f_half, hidden), BF16),
        pltpu.VMEM((2, f_half, hidden), BF16),
        pltpu.VMEM((2, X, f_x, hidden), BF16),
        pltpu.VMEM((2, f_x, hidden), BF16),
        pltpu.VMEM((2, z_n, piece, hidden), BF16),
        pltpu.VMEM((2, y_n, piece, hidden), BF16),
        pltpu.VMEM((2, width, hidden), BF16),
        pltpu.VMEM((2, 8, hidden), F32),
        pltpu.VMEM((X, 8, hidden), F32),
        pltpu.VMEM((z_n, 8, hidden), F32),
        pltpu.VMEM((y_n, 8, hidden), F32),
        pltpu.VMEM((8, LANES), jnp.int32),
        pltpu.SMEM((8, LANES), jnp.int32),
        pltpu.SemaphoreType.DMA((10,)),
        pltpu.SemaphoreType.DMA((5,)),
        pltpu.SemaphoreType.DMA((SEND_POOL,)),
        pltpu.SemaphoreType.DMA((copies,)),
    ]
    shapes = (
            jax.ShapeDtypeStruct((nodes_dev, hidden), BF16),
            jax.ShapeDtypeStruct((nodes_dev, width), BF16),
            jax.ShapeDtypeStruct((width, hidden), BF16),
            jax.ShapeDtypeStruct((width, hidden), BF16),
            jax.ShapeDtypeStruct((1, hidden), F32),
        )
    results = pl.pallas_call(
        functools.partial(kernel, rows, cols, slots, scale),
        out_shape=shapes,
        in_specs=[hbm] * 9,
        out_specs=[hbm] * 5,
        scratch_shapes=scratch,
        compiler_params=pltpu.CompilerParams(
            collective_id=0, has_side_effects=True, vmem_limit_bytes=60 * 1024 * 1024
        ),
    )(
        features, degree.reshape(1, nodes_dev), blocks.reshape(slots, side, side),
        coords.reshape(1, slots), counts, w_self, w_neigh, offset.reshape(hidden // LANES, LANES), cotangent,
    )
    node_out, feat_grad, self_grad, neigh_grad, offset_grad = pl.pallas_call(
        hand_on,
        out_shape=shapes,
        in_specs=[hbm] * 5,
        out_specs=[hbm] * 5,
        scratch_shapes=[pltpu.VMEM(held.shape, held.dtype) for held in shapes]
        + [pltpu.SemaphoreType.DMA((5,)), pltpu.SemaphoreType.DMA((5,))],
        compiler_params=pltpu.CompilerParams(vmem_limit_bytes=60 * 1024 * 1024),
    )(*results)
    return node_out, feat_grad, self_grad, neigh_grad, offset_grad.reshape(hidden)


def solution(mesh):
    return jax.shard_map(
        functools.partial(run, mesh.shape["row"], mesh.shape["col"]),
        mesh=mesh,
        in_specs=(
            P(("row", "col"), None),
            P(("row", "col")),
            P("row", "col", None, None, None),
            P("row", "col", None),
            P("row", "col"),
            P(),
            P(),
            P(),
            P(("row", "col"), None),
        ),
        out_specs=(P(("row", "col"), None), P(("row", "col"), None), P(), P(), P()),
        check_vma=False,
    )
```
